256 devices in a mesh: inputs: 64 (over x_hi, y, z), tm: 4 (over x_lo, core).
Axes of the slice: x: 4 (x_hi: 2, x_lo: 2; x = x_hi * 2 + x_lo), y: 4, z: 8, core: 2. Of those that a mesh axis runs over, the one named last changes fastest.
Arguments:
- voltages: bfloat16 [1024, 131072], P('inputs', 'tm'), may hold values from -8 to 8
- pfb_taps: float32 [8, 512], replicated, may hold values from -2 to 2
Outputs:
- visibilities: float32 [256, 36, 2, 128, 128], P(('inputs', 'tm'))
The draws below stay inside these ranges and needn't reach their ends.
All inputs are finite; a program needn't handle non-finite values.
Results may differ from the reference program's by a relative error of at most 0.002.
Values may be sent and summed in bfloat16 or wider, within the bound.
A program may use at most 128 MiB of HBM per device.

```python
import jax
import jax.numpy as jnp
from jax import lax

F = 256
TAPS = 8
TILE = 128
FRAME = 512
INPUTS = 1024
FRAMES = 256
SAMPLES = 131072
NT = 8


def draw_voltages(key, part):
    base = jax.random.fold_in(key, 7)
    key_sky, key_gain, key_noise = jax.random.split(base, 3)
    sky = jax.random.normal(key_sky, (1, SAMPLES), jnp.float32)
    gain = jax.random.uniform(key_gain, (INPUTS, 1), jnp.float32, 0.3, 0.9)
    noise = jax.random.normal(key_noise, (INPUTS, SAMPLES), jnp.float32)
    values = gain * sky + noise
    return jnp.clip(values, -8.0, 8.0).astype(jnp.bfloat16)


def centred(rng, shape, scale, reach, held_as=jnp.bfloat16):
    return jnp.clip(scale * jax.random.normal(rng, shape, jnp.float32), -reach, reach).astype(held_as)


def setup_inputs(seed: int = 0) -> dict:
    key_of = jax.random.split(jax.random.key(seed), 3)
    return {
        "voltages": draw_voltages(jax.random.fold_in(key_of[2], 71), 0),
        "pfb_taps": centred(key_of[1], (TAPS, FRAME), TAPS ** -0.5, 2.0, jnp.float32),
    }


def dft_table(chans, length):
    rows = jnp.arange(2 * chans, dtype=jnp.int32)
    freq = rows // 2
    part = rows % 2
    samp = jnp.arange(length, dtype=jnp.int32)
    phase = (freq[:, None] * samp[None, :]) % length
    angle = (2.0 * jnp.pi / length) * phase.astype(jnp.float32)
    vals = jnp.where(part[:, None] == 0, jnp.cos(angle), -jnp.sin(angle))
    return (vals * (1.0 / (length ** 0.5))).astype(jnp.bfloat16)


def channelize(group, pfb_taps, table):
    zeros = jnp.zeros((TILE, TAPS - 1, FRAME), jnp.bfloat16)
    extended = jnp.concatenate([zeros, group], axis=1)
    filtered = jnp.zeros((TILE, FRAMES, FRAME), jnp.float32)
    for tap in range(TAPS):
        filtered = filtered + pfb_taps[tap][None, None, :] * extended[:, tap:tap + FRAMES, :].astype(jnp.float32)
    rounded = lax.optimization_barrier(filtered.astype(jnp.bfloat16)).astype(jnp.float32)
    spec = jnp.einsum("kn,itn->kit", table.astype(jnp.float32), rounded)
    return spec.astype(jnp.bfloat16)


def channel_tiles(spec):
    left = jnp.concatenate([spec[0], spec[1]], axis=-1)
    twisted = jnp.concatenate([spec[1], -spec[0]], axis=-1)
    real_rows = []
    imag_rows = []
    for first in range(NT):
        lo = first * TILE
        cols = left[lo:]
        real_part = jnp.dot(left[lo:lo + TILE], cols.T, preferred_element_type=jnp.float32)
        imag_part = jnp.dot(twisted[lo:lo + TILE], cols.T, preferred_element_type=jnp.float32)
        count = NT - first
        real_rows.append(real_part.reshape(TILE, count, TILE).transpose(1, 0, 2))
        imag_rows.append(imag_part.reshape(TILE, count, TILE).transpose(1, 0, 2))
    real_all = jnp.concatenate(real_rows, axis=0)
    imag_all = jnp.concatenate(imag_rows, axis=0)
    return jnp.stack([real_all, imag_all], axis=1) * (1.0 / FRAMES)


def reference(voltages, pfb_taps):
    table = dft_table(F, FRAME)
    groups = voltages.reshape(NT, TILE, FRAMES, FRAME)
    spectra = lax.map(lambda group: channelize(group, pfb_taps, table), groups)
    spectra = spectra.transpose(1, 0, 2, 3).reshape(F, 2, INPUTS, FRAMES)
    return lax.map(channel_tiles, spectra)
```

```python
import functools

import jax
import jax.numpy as jnp
import numpy as np
from jax import lax
from jax.experimental import pallas as pl
from jax.experimental.pallas import tpu as pltpu
from jax.sharding import PartitionSpec as P

F = 256
TAPS = 8
TILE = 128
FRAME = 512
HALO = (TAPS - 1) * FRAME
LANES = 128
MESH = pl.DeviceIdType.MESH


def dft_table(chans, length, owners):
    freq = np.arange(chans, dtype=np.int32)
    samp = np.arange(length, dtype=np.int32)
    phase = (freq[:, None] * samp[None, :]) % length
    angle = 2.0 * np.pi / length * phase.astype(np.float64)
    vals = np.stack([np.cos(angle), -np.sin(angle)]) / length**0.5
    vals = vals.reshape(2, chans // owners, owners, length).transpose(2, 0, 1, 3)
    return vals.reshape(2 * chans, length).astype(np.float32).astype(jnp.bfloat16)


def grid_coords():
    along = lax.axis_index("inputs")
    block = lax.axis_index("tm")
    return along // 32, (along // 8) % 4, along % 8, block


def grid_device(x_hi, y, z, block):
    return (x_hi * 32 + y * 8 + z, block)


def channel_kernel(
    frames, v_hbm, taps_ref, table_hbm, recv,
    volts, table, halo, filt32, filt, stage, send,
    in_sems, halo_send, halo_recv, send_sem, recv_sem, y_sem, x_sem,
):
    x_hi, y, z, block = grid_coords()
    blocks = 4
    groups = 64
    inp = v_hbm.shape[0]

    load_volts = pltpu.make_async_copy(v_hbm, volts, in_sems.at[0])
    load_table = pltpu.make_async_copy(table_hbm, table, in_sems.at[1])
    load_volts.start()
    load_table.start()

    barrier = pltpu.get_barrier_semaphore()
    z_peers = [grid_device(x_hi, y, lax.rem(z + d, 8), block) for d in range(1, 8)]
    y_peers = [grid_device(x_hi, lax.rem(y + d, 4), z, block) for d in range(1, 4)]
    x_peers = [
        grid_device(lax.rem(x_hi + d // 4, 2), y, z, lax.rem(block + d % 4, 4)) for d in range(1, 8)
    ]
    for peer in x_peers + y_peers + z_peers:
        pl.semaphore_signal(barrier, inc=1, device_id=peer, device_id_type=MESH)

    load_volts.wait()

    def filter_frames(first, read):
        for part in range(FRAME // LANES):
            lane = part * LANES
            rows = [read(d, lane).astype(jnp.float32) for d in range(-(TAPS - 1), TAPS)]
            taps = [taps_ref[p : p + 1, lane : lane + LANES] for p in range(TAPS)]
            for t in range(TAPS):
                total = taps[0] * rows[t]
                for p in range(1, TAPS):
                    total = total + taps[p] * rows[t + p]
                for half in range(2):
                    filt32[part, pl.ds(half * frames + first + t, 8, stride=2 * frames), :] = total[
                        half * 8 : half * 8 + 8
                    ]

    def read_volts(first):
        def read(d, lane):
            start = pl.multiple_of((first + d) * FRAME, FRAME) + lane
            return volts[:, pl.ds(start, LANES)]

        return read

    def filter_blocks(low, high):
        @pl.loop(low, high)
        def _(b):
            first = pl.multiple_of(b * TAPS, TAPS)
            filter_frames(first, read_volts(first))

    halo_copy = pltpu.make_async_remote_copy(
        src_ref=volts.at[:, pl.ds(frames * FRAME - HALO, HALO)],
        dst_ref=halo,
        send_sem=halo_send,
        recv_sem=halo_recv,
        device_id=(lax.axis_index("inputs"), lax.rem(block + 1, blocks)),
        device_id_type=MESH,
    )

    filter_blocks(1, 4)
    pl.semaphore_wait(barrier, len(x_peers + y_peers + z_peers))

    @pl.when(block < blocks - 1)
    def _():
        halo_copy.start()

    for peer in y_peers:
        pl.semaphore_signal(y_sem, inc=1, device_id=peer, device_id_type=MESH)
    filter_blocks(4, 6)
    pl.semaphore_wait(y_sem, len(y_peers))
    for peer in x_peers:
        pl.semaphore_signal(x_sem, inc=1, device_id=peer, device_id_type=MESH)
    filter_blocks(6, frames // TAPS)

    @pl.when(block > 0)
    def _():
        halo_copy.wait_recv()

    @pl.when(block == 0)
    def _():
        halo[...] = jnp.zeros_like(halo)

    def read_first(d, lane):
        if d < 0:
            return halo[:, (d + TAPS - 1) * FRAME + lane : (d + TAPS - 1) * FRAME + lane + LANES]
        return volts[:, d * FRAME + lane : d * FRAME + lane + LANES]

    filter_frames(0, read_first)
    for part in range(FRAME // LANES):
        filt[:, part * LANES : (part + 1) * LANES] = filt32[part].astype(jnp.bfloat16)
    load_table.wait()

    low = lax.broadcasted_iota(jnp.int32, (8, LANES), 1) < LANES // 2

    me = lax.axis_index("inputs")
    slot = pl.multiple_of((block * groups + me) * inp, inp)

    def transform(j):
        owner = lax.rem(block + j, blocks)
        rows = table[pl.ds(pl.multiple_of(owner * 2 * groups, 2 * groups), 2 * groups), :]
        for q in range(4):
            spec = lax.dot_general(
                rows,
                filt[q * 256 : (q + 1) * 256, :],
                (((1,), (1,)), ((), ())),
                preferred_element_type=jnp.float32,
            )
            for u in range(2):
                pair = 2 * q + u
                for g in range(groups // 8):
                    re = spec[g * 8 : g * 8 + 8, u * LANES : (u + 1) * LANES]
                    im = spec[groups + g * 8 : groups + g * 8 + 8, u * LANES : (u + 1) * LANES]
                    first = jnp.where(low, re, pltpu.roll(im, LANES // 2, 1))
                    second = jnp.where(low, pltpu.roll(re, LANES // 2, 1), im)
                    base = g * 8 * inp + pair
                    stage[pl.ds(base, 8, stride=inp), :] = first
                    stage[pl.ds(base + 8, 8, stride=inp), :] = second
        send[j] = stage[...].astype(jnp.bfloat16)

    def copy_to(j, device, row):
        return pltpu.make_async_remote_copy(
            src_ref=send.at[j, pl.ds(pl.multiple_of(row * inp, inp), inp)],
            dst_ref=recv.at[pl.ds(slot, inp)],
            send_sem=send_sem,
            recv_sem=recv_sem,
            device_id=device,
            device_id_type=MESH,
        )

    for j in range(blocks):
        transform(j)
        if j == 0:
            pl.semaphore_wait(x_sem, len(x_peers))

        @pl.loop(1 if j == 0 else 0, groups)
        def _(s):
            tx = lax.rem(x_hi + s // 32, 2)
            ty = lax.rem(y + (s // 8) % 4, 4)
            tz = lax.rem(z + s % 8, 8)
            row = tx * 32 + ty * 8 + tz
            copy_to(j, (row, lax.rem(block + j, blocks)), row).start()

        if j == 0:
            recv[pl.ds(slot, inp), :] = send[0, pl.ds(pl.multiple_of(me * inp, inp), inp), :]

    @pl.when(block < blocks - 1)
    def _():
        halo_copy.wait_send()

    count = (blocks * groups - 1) * inp
    drain = pltpu.make_async_remote_copy(
        src_ref=recv.at[pl.ds(0, count)],
        dst_ref=recv.at[pl.ds(0, count)],
        send_sem=send_sem,
        recv_sem=recv_sem,
        device_id=(me, lax.rem(block + 1, blocks)),
        device_id_type=MESH,
    )
    drain.wait_send()
    drain.wait_recv()


def channelize(voltages, pfb_taps, table):
    inp, samples = voltages.shape
    frames = samples // FRAME
    rows = inp * frames
    return pl.pallas_call(
        functools.partial(channel_kernel, frames),
        out_shape=jax.ShapeDtypeStruct((256 * inp, LANES), jnp.bfloat16),
        in_specs=[
            pl.BlockSpec(memory_space=pl.ANY),
            pl.BlockSpec(memory_space=pltpu.VMEM),
            pl.BlockSpec(memory_space=pl.ANY),
        ],
        out_specs=pl.BlockSpec(memory_space=pltpu.VMEM),
        scratch_shapes=[
            pltpu.VMEM((inp, samples), jnp.bfloat16),
            pltpu.VMEM((2 * F, FRAME), jnp.bfloat16),
            pltpu.VMEM((inp, HALO), jnp.bfloat16),
            pltpu.VMEM((FRAME // LANES, rows, LANES), jnp.float32),
            pltpu.VMEM((rows, FRAME), jnp.bfloat16),
            pltpu.VMEM((64 * inp, LANES), jnp.float32),
            pltpu.VMEM((4, 64 * inp, LANES), jnp.bfloat16),
            pltpu.SemaphoreType.DMA((2,)),
            pltpu.SemaphoreType.DMA,
            pltpu.SemaphoreType.DMA,
            pltpu.SemaphoreType.DMA,
            pltpu.SemaphoreType.DMA,
            pltpu.SemaphoreType.REGULAR,
            pltpu.SemaphoreType.REGULAR,
        ],
        compiler_params=pltpu.CompilerParams(
            collective_id=0, has_side_effects=True, vmem_limit_bytes=32 << 20
        ),
    )(voltages, pfb_taps, table)


def tile_kernel(scale, spec_ref, out_hbm, tiles, sem):
    blocks, count_in, lanes = spec_ref.shape
    nt = count_in // TILE
    left = jnp.concatenate([spec_ref[b] for b in range(blocks)], axis=-1)
    sign = jnp.where(lax.broadcasted_iota(jnp.int32, (1, lanes), 1) < lanes // 2, 1.0, -1.0)
    side = 2 * TILE
    copies = []
    pair = 0
    for big in range(nt // 2):
        rows = slice(big * side, (big + 1) * side)
        twisted = jnp.concatenate(
            [
                (pltpu.roll(spec_ref[b, rows].astype(jnp.float32), lanes // 2, 1) * sign).astype(
                    jnp.bfloat16
                )
                for b in range(blocks)
            ],
            axis=-1,
        )
        both = jnp.concatenate([left[rows], twisted], axis=0)
        first_pair = pair
        for cb in range(big, nt // 2):
            prod = lax.dot_general(
                both,
                left[cb * side : (cb + 1) * side],
                (((1,), (1,)), ((), ())),
                preferred_element_type=jnp.float32,
            ) * scale
            for a in range(2):
                for b in range(2):
                    row, col = 2 * big + a, 2 * cb + b
                    if col < row:
                        continue
                    place = row * nt - row * (row - 1) // 2 + col - row
                    for c in range(2):
                        lo = c * side + a * TILE
                        tiles[place, c] = prod[lo : lo + TILE, b * TILE : (b + 1) * TILE]
        pair = (2 * big + 2) * nt - (2 * big + 2) * (2 * big + 1) // 2
        copy = pltpu.make_async_copy(
            tiles.at[first_pair:pair], out_hbm.at[0, first_pair:pair], sem.at[big]
        )
        copy.start()
        copies.append(copy)
    for copy in copies:
        copy.wait()


def tile_sums(spec, scale):
    nt = spec.shape[1] // TILE
    pairs = nt * (nt + 1) // 2
    return pl.pallas_call(
        functools.partial(tile_kernel, scale),
        out_shape=jax.ShapeDtypeStruct((1, pairs, 2, TILE, TILE), jnp.float32),
        in_specs=[pl.BlockSpec(memory_space=pltpu.VMEM)],
        out_specs=pl.BlockSpec(memory_space=pl.ANY),
        scratch_shapes=[
            pltpu.VMEM((pairs, 2, TILE, TILE), jnp.float32),
            pltpu.SemaphoreType.DMA((nt // 2,)),
        ],
        compiler_params=pltpu.CompilerParams(vmem_limit_bytes=32 << 20),
    )(spec)


def on_device(voltages, pfb_taps):
    table = jnp.asarray(dft_table(F, FRAME, lax.axis_size("tm")))
    frames = voltages.shape[1] // FRAME
    turned = channelize(voltages, pfb_taps, table)
    spec = turned.reshape(lax.axis_size("tm"), lax.axis_size("inputs") * voltages.shape[0], LANES)
    return tile_sums(spec, 1.0 / (frames * lax.axis_size("tm")))


def solution(mesh):
    in_specs = (P("inputs", "tm"), P())
    out_specs = P(("inputs", "tm"), None, None, None, None)
    return jax.shard_map(
        on_device, mesh=mesh, in_specs=in_specs, out_specs=out_specs, check_vma=False
    )
```

```python
import functools

import jax
import jax.numpy as jnp
import numpy as np
from jax import lax
from jax.experimental import pallas as pl
from jax.experimental.pallas import tpu as pltpu
from jax.sharding import PartitionSpec as P

F = 256
TAPS = 8
TILE = 128
FRAME = 512
HALO = (TAPS - 1) * FRAME
LANES = 128
CHUNKS = 4
TABLE_COPIES = 3
VMEM_BYTES = 55312384
MESH = pl.DeviceIdType.MESH


def dft_table(chans, length, owners):
    freq = np.arange(chans, dtype=np.int32)
    samp = np.arange(length, dtype=np.int32)
    phase = (freq[:, None] * samp[None, :]) % length
    angle = 2.0 * np.pi / length * phase.astype(np.float64)
    vals = np.stack([np.cos(angle), -np.sin(angle)]) / length**0.5
    vals = vals.reshape(2, chans // owners, owners, length).transpose(2, 0, 1, 3)
    vals = vals.reshape(2 * chans, length).astype(np.float32).astype(jnp.bfloat16)
    return np.concatenate([vals] * TABLE_COPIES)


def grid_coords():
    along = lax.axis_index("inputs")
    block = lax.axis_index("tm")
    return along // 32, (along // 8) % 4, along % 8, block


def grid_device(x_hi, y, z, block):
    return (x_hi * 32 + y * 8 + z, block)


def channel_kernel(
    frames, v_hbm, taps_hbm, table_hbm, recv,
    volts, taps_ref, table, halo, filt32, filt, stage, send,
    in_sems, halo_send, halo_recv, send_sem, recv_sem, y_sem, x_sem,
):
    x_hi, y, z, block = grid_coords()
    blocks = 4
    groups = 64
    inp = v_hbm.shape[0]

    chunk = frames // CHUNKS
    load_volts = []
    for c in range(CHUNKS):
        part = pl.ds(c * chunk * FRAME, chunk * FRAME)
        load_volts.append(pltpu.make_async_copy(v_hbm.at[:, part], volts.at[:, part], in_sems.at[c]))
    load_taps = pltpu.make_async_copy(taps_hbm, taps_ref, in_sems.at[CHUNKS])
    load_table = pltpu.make_async_copy(table_hbm.at[0 : 2 * F], table, in_sems.at[CHUNKS + 1])
    load_taps.start()
    for load in load_volts:
        load.start()

    barrier = pltpu.get_barrier_semaphore()
    z_peers = [grid_device(x_hi, y, lax.rem(z + d, 8), block) for d in range(1, 8)]
    y_peers = [grid_device(x_hi, lax.rem(y + d, 4), z, block) for d in range(1, 4)]
    x_peers = [
        grid_device(lax.rem(x_hi + d // 4, 2), y, z, lax.rem(block + d % 4, 4)) for d in range(1, 8)
    ]
    for peer in z_peers + y_peers + x_peers:
        pl.semaphore_signal(barrier, inc=1, device_id=peer, device_id_type=MESH)

    load_table.start()
    load_taps.wait()

    def filter_frames(first, read):
        for part in range(FRAME // LANES):
            lane = part * LANES
            rows = [read(d, lane).astype(jnp.float32) for d in range(-(TAPS - 1), TAPS)]
            taps = [taps_ref[p : p + 1, lane : lane + LANES] for p in range(TAPS)]
            for t in range(TAPS):
                total = taps[0] * rows[t]
                for p in range(1, TAPS):
                    total = total + taps[p] * rows[t + p]
                for half in range(2):
                    filt32[part, pl.ds(half * frames + first + t, 8, stride=2 * frames), :] = total[
                        half * 8 : half * 8 + 8
                    ]

    def read_volts(first):
        def read(d, lane):
            start = pl.multiple_of((first + d) * FRAME, FRAME) + lane
            return volts[:, pl.ds(start, LANES)]

        return read

    def filter_blocks(low, high):
        @pl.loop(low, high)
        def _(b):
            first = pl.multiple_of(b * TAPS, TAPS)
            filter_frames(first, read_volts(first))

    halo_copy = pltpu.make_async_remote_copy(
        src_ref=v_hbm.at[:, pl.ds(frames * FRAME - HALO, HALO)],
        dst_ref=halo,
        send_sem=halo_send,
        recv_sem=halo_recv,
        device_id=(lax.axis_index("inputs"), lax.rem(block + 1, blocks)),
        device_id_type=MESH,
    )

    load_volts[0].wait()
    pl.semaphore_wait(barrier, len(x_peers + y_peers + z_peers))

    @pl.when(block < blocks - 1)
    def _():
        halo_copy.start()

    for peer in y_peers:
        pl.semaphore_signal(y_sem, inc=1, device_id=peer, device_id_type=MESH)
    per = chunk // TAPS
    filter_blocks(1, per)
    for c in range(1, CHUNKS):
        load_volts[c].wait()
        filter_blocks(c * per, (c + 1) * per)
    pl.semaphore_wait(y_sem, len(y_peers))
    for peer in x_peers:
        pl.semaphore_signal(x_sem, inc=1, device_id=peer, device_id_type=MESH)

    @pl.when(block > 0)
    def _():
        halo_copy.wait_recv()

    @pl.when(block == 0)
    def _():
        halo[...] = jnp.zeros_like(halo)

    def read_first(d, lane):
        if d < 0:
            return halo[:, (d + TAPS - 1) * FRAME + lane : (d + TAPS - 1) * FRAME + lane + LANES]
        return volts[:, d * FRAME + lane : d * FRAME + lane + LANES]

    filter_frames(0, read_first)
    load_table.wait()

    low = lax.broadcasted_iota(jnp.int32, (8, LANES), 1) < LANES // 2

    me = lax.axis_index("inputs")
    slot = pl.multiple_of((block * groups + me) * inp, inp)

    def transform(j):
        owner = lax.rem(block + j, blocks)
        rows = table[pl.ds(pl.multiple_of(owner * 2 * groups, 2 * groups), 2 * groups), :]
        for q in range(4):
            quarter = slice(q * 256, (q + 1) * 256)
            if j == 0:
                filt[quarter, :] = jnp.concatenate(
                    [filt32[part, quarter, :] for part in range(FRAME // LANES)], axis=1
                ).astype(jnp.bfloat16)
            spec = lax.dot_general(
                rows,
                filt[quarter, :],
                (((1,), (1,)), ((), ())),
                preferred_element_type=jnp.float32,
            )
            for u in range(2):
                pair = 2 * q + u
                for g in range(groups // 8):
                    re = spec[g * 8 : g * 8 + 8, u * LANES : (u + 1) * LANES]
                    im = spec[groups + g * 8 : groups + g * 8 + 8, u * LANES : (u + 1) * LANES]
                    first = jnp.where(low, re, pltpu.roll(im, LANES // 2, 1))
                    second = jnp.where(low, pltpu.roll(re, LANES // 2, 1), im)
                    base = g * 8 * inp + pair
                    stage[pl.ds(base, 8, stride=inp), :] = first
                    stage[pl.ds(base + 8, 8, stride=inp), :] = second
        send[j] = stage[...].astype(jnp.bfloat16)

    def copy_to(j, device, row):
        return pltpu.make_async_remote_copy(
            src_ref=send.at[j, pl.ds(pl.multiple_of(row * inp, inp), inp)],
            dst_ref=recv.at[pl.ds(slot, inp)],
            send_sem=send_sem,
            recv_sem=recv_sem,
            device_id=device,
            device_id_type=MESH,
        )

    def send_range(j, low_step, high_step, turn):
        @pl.loop(low_step, high_step)
        def _(s):
            tx = lax.rem(x_hi + s // 32 + turn * (s // 4), 2)
            ty = lax.rem(y + s // 8 + s, 4)
            tz = lax.rem(z + s, 8)
            row = tx * 32 + ty * 8 + tz
            copy_to(j, (row, lax.rem(block + j, blocks)), row).start()

    for j in range(blocks):
        transform(j)
        if j == 0:
            send_range(j, 1, groups // 2, 0)
            pl.semaphore_wait(x_sem, len(x_peers))
            send_range(j, groups // 2, groups, 0)
            recv[pl.ds(slot, inp), :] = send[0, pl.ds(pl.multiple_of(me * inp, inp), inp), :]
        else:
            send_range(j, 0, groups, 1)

    @pl.when(block < blocks - 1)
    def _():
        halo_copy.wait_send()

    count = (blocks * groups - 1) * inp
    drain = pltpu.make_async_remote_copy(
        src_ref=recv.at[pl.ds(0, count)],
        dst_ref=recv.at[pl.ds(0, count)],
        send_sem=send_sem,
        recv_sem=recv_sem,
        device_id=(me, lax.rem(block + 1, blocks)),
        device_id_type=MESH,
    )
    drain.wait_send()
    drain.wait_recv()


def channelize(voltages, pfb_taps, table):
    inp, samples = voltages.shape
    frames = samples // FRAME
    rows = inp * frames
    return pl.pallas_call(
        functools.partial(channel_kernel, frames),
        out_shape=jax.ShapeDtypeStruct((256 * inp, LANES), jnp.bfloat16),
        in_specs=[
            pl.BlockSpec(memory_space=pltpu.HBM),
            pl.BlockSpec(memory_space=pltpu.HBM),
            pl.BlockSpec(memory_space=pltpu.HBM),
        ],
        out_specs=pl.BlockSpec(memory_space=pltpu.VMEM),
        scratch_shapes=[
            pltpu.VMEM((inp, samples), jnp.bfloat16),
            pltpu.VMEM((TAPS, FRAME), jnp.float32),
            pltpu.VMEM((2 * F, FRAME), jnp.bfloat16),
            pltpu.VMEM((inp, HALO), jnp.bfloat16),
            pltpu.VMEM((FRAME // LANES, rows, LANES), jnp.float32),
            pltpu.VMEM((rows, FRAME), jnp.bfloat16),
            pltpu.VMEM((64 * inp, LANES), jnp.float32),
            pltpu.VMEM((4, 64 * inp, LANES), jnp.bfloat16),
            pltpu.SemaphoreType.DMA((CHUNKS + 2,)),
            pltpu.SemaphoreType.DMA,
            pltpu.SemaphoreType.DMA,
            pltpu.SemaphoreType.DMA,
            pltpu.SemaphoreType.DMA,
            pltpu.SemaphoreType.REGULAR,
            pltpu.SemaphoreType.REGULAR,
        ],
        compiler_params=pltpu.CompilerParams(
            collective_id=0, has_side_effects=True, vmem_limit_bytes=VMEM_BYTES
        ),
    )(voltages, pfb_taps, table)


def tile_kernel(scale, spec_ref, out_hbm, tiles, sem):
    blocks, count_in, lanes = spec_ref.shape
    nt = count_in // TILE
    left = jnp.concatenate([spec_ref[b] for b in range(blocks)], axis=-1)
    sign = jnp.where(lax.broadcasted_iota(jnp.int32, (1, lanes), 1) < lanes // 2, 1.0, -1.0)
    side = 2 * TILE
    copies = []
    for big in range(nt // 2):
        rows = slice(big * side, (big + 1) * side)
        twisted = jnp.concatenate(
            [
                (pltpu.roll(spec_ref[b, rows].astype(jnp.float32), lanes // 2, 1) * sign).astype(
                    jnp.bfloat16
                )
                for b in range(blocks)
            ],
            axis=-1,
        )
        both = jnp.concatenate([left[rows], twisted], axis=0)
        for cb in range(big, nt // 2):
            prod = lax.dot_general(
                both,
                left[cb * side : (cb + 1) * side],
                (((1,), (1,)), ((), ())),
                preferred_element_type=jnp.float32,
            ) * scale
            for a in range(2):
                for b in range(2):
                    row, col = 2 * big + a, 2 * cb + b
                    if col < row:
                        continue
                    place = row * nt - row * (row - 1) // 2 + col - row
                    for c in range(2):
                        lo = c * side + a * TILE
                        tiles[place, c] = prod[lo : lo + TILE, b * TILE : (b + 1) * TILE]
                first = max(row, 2 * cb)
                place = row * nt - row * (row - 1) // 2 + first - row
                pairs = slice(place, place + 2 * cb + 2 - first)
                copy = pltpu.make_async_copy(
                    tiles.at[pairs], out_hbm.at[0, pairs], sem.at[len(copies)]
                )
                copy.start()
                copies.append(copy)
    for copy in copies:
        copy.wait()


def tile_sums(spec, scale):
    nt = spec.shape[1] // TILE
    pairs = nt * (nt + 1) // 2
    return pl.pallas_call(
        functools.partial(tile_kernel, scale),
        out_shape=jax.ShapeDtypeStruct((1, pairs, 2, TILE, TILE), jnp.float32),
        in_specs=[pl.BlockSpec(memory_space=pltpu.VMEM)],
        out_specs=pl.BlockSpec(memory_space=pl.ANY),
        scratch_shapes=[
            pltpu.VMEM((pairs, 2, TILE, TILE), jnp.float32),
            pltpu.SemaphoreType.DMA((nt // 2 * (nt // 2 + 1),)),
        ],
        compiler_params=pltpu.CompilerParams(vmem_limit_bytes=32 << 20),
    )(spec)


def on_device(voltages, pfb_taps):
    table = jnp.asarray(dft_table(F, FRAME, lax.axis_size("tm")))
    frames = voltages.shape[1] // FRAME
    turned = channelize(voltages, pfb_taps, table)
    spec = turned.reshape(lax.axis_size("tm"), lax.axis_size("inputs") * voltages.shape[0], LANES)
    return tile_sums(spec, 1.0 / (frames * lax.axis_size("tm")))


def solution(mesh):
    in_specs = (P("inputs", "tm"), P())
    out_specs = P(("inputs", "tm"), None, None, None, None)
    return jax.shard_map(
        on_device, mesh=mesh, in_specs=in_specs, out_specs=out_specs, check_vma=False
    )
```

```python
import functools

import jax
import jax.numpy as jnp
import numpy as np
from jax import lax
from jax.experimental import pallas as pl
from jax.experimental.pallas import tpu as pltpu
from jax.sharding import PartitionSpec as P

F = 256
TAPS = 8
TILE = 128
FRAME = 512
HALO = (TAPS - 1) * FRAME
LANES = 128
CHUNKS = 8
EARLY = 3
PITCH = 136
PARTS = 6
TABLE_COPIES = 3
VMEM_BYTES = 51298304
MESH = pl.DeviceIdType.MESH


def dft_table(chans, length, owners):
    freq = np.arange(chans, dtype=np.int32)
    samp = np.arange(length, dtype=np.int32)
    phase = (freq[:, None] * samp[None, :]) % length
    angle = 2.0 * np.pi / length * phase.astype(np.float64)
    vals = np.stack([np.cos(angle), -np.sin(angle)]) / length**0.5
    vals = vals.reshape(2, chans // owners, owners, length).transpose(2, 0, 1, 3)
    vals = vals.reshape(2 * chans, length).astype(np.float32).astype(jnp.bfloat16)
    return np.concatenate([vals] * TABLE_COPIES)


def grid_coords():
    along = lax.axis_index("inputs")
    block = lax.axis_index("tm")
    return along // 32, (along // 8) % 4, along % 8, block


def grid_device(x_hi, y, z, block):
    return (x_hi * 32 + y * 8 + z, block)


def channel_kernel(
    frames, v_hbm, taps_hbm, table_hbm, late, *refs
):
    sums = refs[:PARTS]
    (
        volts, taps_ref, table, halo, filt32, filt, stage, send, early,
        in_sems, halo_send, halo_recv, send_sem, recv_sems, y_sem, x_sem,
    ) = refs[PARTS:]
    x_hi, y, z, block = grid_coords()
    blocks = 4
    groups = 64
    inp = v_hbm.shape[0]

    chunk = frames // CHUNKS
    load_volts = []
    for c in range(CHUNKS):
        part = pl.ds(c * chunk * FRAME, chunk * FRAME)
        load_volts.append(pltpu.make_async_copy(v_hbm.at[:, part], volts.at[:, part], in_sems.at[c]))
    load_taps = pltpu.make_async_copy(taps_hbm, taps_ref, in_sems.at[CHUNKS])
    load_table = pltpu.make_async_copy(table_hbm.at[0 : 2 * F], table, in_sems.at[CHUNKS + 1])
    load_taps.start()
    for load in load_volts:
        load.start()

    barrier = pltpu.get_barrier_semaphore()
    z_peers = [grid_device(x_hi, y, lax.rem(z + d, 8), block) for d in range(1, 8)]
    y_peers = [grid_device(x_hi, lax.rem(y + d, 4), z, block) for d in range(1, 4)]
    x_peers = [
        grid_device(lax.rem(x_hi + d // 4, 2), y, z, lax.rem(block + d % 4, 4)) for d in range(1, 8)
    ]
    for peer in x_peers + z_peers + y_peers:
        pl.semaphore_signal(barrier, inc=1, device_id=peer, device_id_type=MESH)

    load_table.start()

    def filter_frames(first, read):
        for part in range(FRAME // LANES):
            lane = part * LANES
            rows = [read(d, lane).astype(jnp.float32) for d in range(-(TAPS - 1), TAPS)]
            taps = [taps_ref[p : p + 1, lane : lane + LANES] for p in range(TAPS)]
            for t in range(TAPS):
                total = taps[0] * rows[t]
                for p in range(1, TAPS):
                    total = total + taps[p] * rows[t + p]
                for half in range(2):
                    filt32[part, pl.ds(half * frames + first + t, 8, stride=PITCH), :] = total[
                        half * 8 : half * 8 + 8
                    ]

    def read_volts(first):
        def read(d, lane):
            start = pl.multiple_of((first + d) * FRAME, FRAME) + lane
            return volts[:, pl.ds(start, LANES)]

        return read

    def filter_blocks(low, high):
        @pl.loop(low, high)
        def _(b):
            first = pl.multiple_of(b * TAPS, TAPS)
            filter_frames(first, read_volts(first))

    halo_copy = pltpu.make_async_remote_copy(
        src_ref=v_hbm.at[:, pl.ds(frames * FRAME - HALO, HALO)],
        dst_ref=halo,
        send_sem=halo_send,
        recv_sem=halo_recv,
        device_id=(lax.axis_index("inputs"), lax.rem(block + 1, blocks)),
        device_id_type=MESH,
    )

    pl.semaphore_wait(barrier, len(x_peers + y_peers + z_peers))

    @pl.when(block < blocks - 1)
    def _():
        halo_copy.start()

    for peer in y_peers:
        pl.semaphore_signal(y_sem, inc=1, device_id=peer, device_id_type=MESH)
    per = chunk // TAPS
    load_taps.wait()
    load_volts[0].wait()
    filter_blocks(1, per)
    for c in range(1, CHUNKS):
        load_volts[c].wait()
        filter_blocks(c * per, (c + 1) * per)
    pl.semaphore_wait(y_sem, len(y_peers))
    for peer in x_peers:
        pl.semaphore_signal(x_sem, inc=1, device_id=peer, device_id_type=MESH)

    @pl.when(block > 0)
    def _():
        halo_copy.wait_recv()

    @pl.when(block == 0)
    def _():
        halo[...] = jnp.zeros_like(halo)

    def read_first(d, lane):
        if d < 0:
            return halo[:, (d + TAPS - 1) * FRAME + lane : (d + TAPS - 1) * FRAME + lane + LANES]
        return volts[:, d * FRAME + lane : d * FRAME + lane + LANES]

    filter_frames(0, read_first)
    load_table.wait()

    low = lax.broadcasted_iota(jnp.int32, (8, LANES), 1) < LANES // 2

    me = lax.axis_index("inputs")
    span = groups * inp
    slot = pl.multiple_of(me * inp, inp)

    def transform(j):
        owner = lax.rem(block + j, blocks)
        rows = table[pl.ds(pl.multiple_of(owner * 2 * groups, 2 * groups), 2 * groups), :]
        for q in range(4):
            quarter = slice(q * 256, (q + 1) * 256)
            if j == 0:
                filt[quarter, :] = jnp.concatenate(
                    [
                        jnp.concatenate(
                            [
                                filt32[part, pair * PITCH : pair * PITCH + 2 * frames, :]
                                for pair in (2 * q, 2 * q + 1)
                            ],
                            axis=0,
                        )
                        for part in range(FRAME // LANES)
                    ],
                    axis=1,
                ).astype(jnp.bfloat16)
            spec = lax.dot_general(
                rows,
                filt[quarter, :],
                (((1,), (1,)), ((), ())),
                preferred_element_type=jnp.float32,
            )
            for u in range(2):
                pair = 2 * q + u
                for g in range(groups // 8):
                    re = spec[g * 8 : g * 8 + 8, u * LANES : (u + 1) * LANES]
                    im = spec[groups + g * 8 : groups + g * 8 + 8, u * LANES : (u + 1) * LANES]
                    first = jnp.where(low, re, pltpu.roll(im, LANES // 2, 1))
                    second = jnp.where(low, pltpu.roll(re, LANES // 2, 1), im)
                    base = g * 8 * inp + pair
                    stage[pl.ds(base, 8, stride=inp), :] = first
                    stage[pl.ds(base + 8, 8, stride=inp), :] = second
        send[j * span : (j + 1) * span, :] = stage[...].astype(jnp.bfloat16)

    def copy_to(j, device, row):
        return pltpu.make_async_remote_copy(
            src_ref=send.at[pl.ds(pl.multiple_of(j * span + row * inp, inp), inp)],
            dst_ref=early.at[pl.ds(j * span + slot, inp)]
            if j < EARLY
            else late.at[j - EARLY, pl.ds(slot, inp)],
            send_sem=send_sem,
            recv_sem=recv_sems.at[0 if j < EARLY else 1],
            device_id=device,
            device_id_type=MESH,
        )

    def send_range(j, low_step, high_step, turn):
        @pl.loop(low_step, high_step)
        def _(s):
            tx = lax.rem(x_hi + s // 32 + turn * (s // 4), 2)
            ty = lax.rem(y + s // 8 + s, 4)
            tz = lax.rem(z + s, 8)
            row = tx * 32 + ty * 8 + tz
            copy_to(j, (row, lax.rem(block + j, blocks)), row).start()

    for j in range(blocks):
        transform(j)
        if j == 0:
            send_range(j, 1, groups // 2, 0)
            pl.semaphore_wait(x_sem, len(x_peers))
            send_range(j, groups // 2, groups, 0)
            early[pl.ds(slot, inp), :] = send[pl.ds(slot, inp), :]
        else:
            send_range(j, 0, groups, 1)

    @pl.when(block < blocks - 1)
    def _():
        halo_copy.wait_send()

    def arrivals(ref, sem):
        return pltpu.make_async_remote_copy(
            src_ref=ref,
            dst_ref=ref,
            send_sem=send_sem,
            recv_sem=recv_sems.at[sem],
            device_id=(me, lax.rem(block + 1, blocks)),
            device_id_type=MESH,
        )

    arrivals(early.at[0 : EARLY * span - inp], 0).wait_recv()

    def keep(place, c, prod):
        sums[place // (36 // PARTS)][place % (36 // PARTS), c] = prod

    tile_products(
        [early.at[j * span : (j + 1) * span] for j in range(EARLY)], keep, lambda *_: None
    )

    arrivals(send.at[0 : blocks * span - inp], 1).wait_send()
    arrivals(late, 1).wait_recv()


def tile_products(specs, keep, done):
    count_in, lanes = specs[0].shape
    nt = count_in // TILE
    left = jnp.concatenate([spec[...] for spec in specs], axis=-1)
    sign = jnp.where(lax.broadcasted_iota(jnp.int32, (1, lanes), 1) < lanes // 2, 1.0, -1.0)
    side = 2 * TILE
    for big in range(nt // 2):
        rows = slice(big * side, (big + 1) * side)
        twisted = jnp.concatenate(
            [
                (pltpu.roll(spec[rows, :].astype(jnp.float32), lanes // 2, 1) * sign).astype(
                    jnp.bfloat16
                )
                for spec in specs
            ],
            axis=-1,
        )
        both = jnp.concatenate([left[rows], twisted], axis=0)
        for cb in range(big, nt // 2):
            prod = lax.dot_general(
                both,
                left[cb * side : (cb + 1) * side],
                (((1,), (1,)), ((), ())),
                preferred_element_type=jnp.float32,
            )
            for a in range(2):
                row = 2 * big + a
                first = max(row, 2 * cb)
                place = row * nt - row * (row - 1) // 2 + first - row
                for col in range(first, 2 * cb + 2):
                    b = col - 2 * cb
                    for c in range(2):
                        lo = c * side + a * TILE
                        keep(
                            place + col - first,
                            c,
                            prod[lo : lo + TILE, b * TILE : (b + 1) * TILE],
                        )
                done(place, place + 2 * cb + 2 - first)


def channelize(voltages, pfb_taps, table):
    inp, samples = voltages.shape
    frames = samples // FRAME
    rows = inp * frames
    return pl.pallas_call(
        functools.partial(channel_kernel, frames),
        out_shape=[jax.ShapeDtypeStruct((4 - EARLY, 64 * inp, LANES), jnp.bfloat16)]
        + [jax.ShapeDtypeStruct((36 // PARTS, 2, TILE, TILE), jnp.float32)] * PARTS,
        in_specs=[
            pl.BlockSpec(memory_space=pltpu.HBM),
            pl.BlockSpec(memory_space=pltpu.HBM),
            pl.BlockSpec(memory_space=pltpu.HBM),
        ],
        out_specs=[pl.BlockSpec(memory_space=pltpu.VMEM)] * (1 + PARTS),
        scratch_shapes=[
            pltpu.VMEM((inp, samples), jnp.bfloat16),
            pltpu.VMEM((TAPS, FRAME), jnp.float32),
            pltpu.VMEM((2 * F, FRAME), jnp.bfloat16),
            pltpu.VMEM((inp, HALO), jnp.bfloat16),
            pltpu.VMEM((FRAME // LANES, 8 * PITCH, LANES), jnp.float32),
            pltpu.VMEM((rows, FRAME), jnp.bfloat16),
            pltpu.VMEM((64 * inp, LANES), jnp.float32),
            pltpu.VMEM((4 * 64 * inp, LANES), jnp.bfloat16),
            pltpu.VMEM((EARLY * 64 * inp, LANES), jnp.bfloat16),
            pltpu.SemaphoreType.DMA((CHUNKS + 2,)),
            pltpu.SemaphoreType.DMA,
            pltpu.SemaphoreType.DMA,
            pltpu.SemaphoreType.DMA,
            pltpu.SemaphoreType.DMA((2,)),
            pltpu.SemaphoreType.REGULAR,
            pltpu.SemaphoreType.REGULAR,
        ],
        compiler_params=pltpu.CompilerParams(
            collective_id=0, has_side_effects=True, vmem_limit_bytes=VMEM_BYTES
        ),
    )(voltages, pfb_taps, table)


def tile_kernel(scale, late, *refs):
    sums = refs[:PARTS]
    out_hbm, tiles, sem = refs[PARTS:]
    copies = []

    def keep(place, c, prod):
        earlier = sums[place // (36 // PARTS)][place % (36 // PARTS), c]
        tiles[place, c] = (earlier + prod) * scale

    def done(low, high):
        copy = pltpu.make_async_copy(
            tiles.at[low:high], out_hbm.at[0, low:high], sem.at[len(copies)]
        )
        copy.start()
        copies.append(copy)

    tile_products([late.at[j] for j in range(late.shape[0])], keep, done)
    for copy in copies:
        copy.wait()


def tile_sums(late, sums, scale):
    nt = late.shape[1] // TILE
    pairs = nt * (nt + 1) // 2
    return pl.pallas_call(
        functools.partial(tile_kernel, scale),
        out_shape=jax.ShapeDtypeStruct((1, pairs, 2, TILE, TILE), jnp.float32),
        in_specs=[pl.BlockSpec(memory_space=pltpu.VMEM)] * (1 + PARTS),
        out_specs=pl.BlockSpec(memory_space=pl.ANY),
        scratch_shapes=[
            pltpu.VMEM((pairs, 2, TILE, TILE), jnp.float32),
            pltpu.SemaphoreType.DMA((nt // 2 * (nt // 2 + 1),)),
        ],
        compiler_params=pltpu.CompilerParams(vmem_limit_bytes=32 << 20),
    )(late, *sums)


def on_device(voltages, pfb_taps):
    table = jnp.asarray(dft_table(F, FRAME, lax.axis_size("tm")))
    frames = voltages.shape[1] // FRAME
    late, *sums = channelize(voltages, pfb_taps, table)
    return tile_sums(late, sums, 1.0 / (frames * lax.axis_size("tm")))


def solution(mesh):
    in_specs = (P("inputs", "tm"), P())
    out_specs = P(("inputs", "tm"), None, None, None, None)
    return jax.shard_map(
        on_device, mesh=mesh, in_specs=in_specs, out_specs=out_specs, check_vma=False
    )
```

```python
import functools

import jax
import jax.numpy as jnp
import numpy as np
from jax import lax
from jax.experimental import pallas as pl
from jax.experimental.pallas import tpu as pltpu
from jax.sharding import PartitionSpec as P

F = 256
TAPS = 8
TILE = 128
FRAME = 512
HALO = (TAPS - 1) * FRAME
LANES = 128
CHUNKS = 8
EARLY = 3
PITCH = 136
PARTS = 6
VMEM_BYTES = 40 << 20
MESH = pl.DeviceIdType.MESH


def dft_table(chans, length, owners):
    freq = np.arange(chans, dtype=np.int32)
    samp = np.arange(length, dtype=np.int32)
    phase = (freq[:, None] * samp[None, :]) % length
    angle = 2.0 * np.pi / length * phase.astype(np.float64)
    vals = np.stack([np.cos(angle), -np.sin(angle)]) / length**0.5
    vals = vals.reshape(2, chans // owners, owners, length).transpose(2, 0, 1, 3)
    vals = vals.reshape(2 * chans, length).astype(np.float32).astype(jnp.bfloat16)
    return vals


def grid_coords():
    along = lax.axis_index("inputs")
    block = lax.axis_index("tm")
    return along // 32, (along // 8) % 4, along % 8, block


def grid_device(x_hi, y, z, block):
    return (x_hi * 32 + y * 8 + z, block)


def channel_kernel(
    frames, v_hbm, taps_hbm, table_hbm, late, *refs
):
    sums = refs[:PARTS]
    (
        volts, taps_ref, table, halo, filt32, filt, stage, send, early,
        in_sems, halo_send, halo_recv, send_sem, recv_sems, y_sem, x_sem,
    ) = refs[PARTS:]
    x_hi, y, z, block = grid_coords()
    blocks = 4
    groups = 64
    inp = v_hbm.shape[0]

    chunk = frames // CHUNKS
    load_volts = []
    for c in range(CHUNKS):
        part = pl.ds(c * chunk * FRAME, chunk * FRAME)
        load_volts.append(pltpu.make_async_copy(v_hbm.at[:, part], volts.at[:, part], in_sems.at[c]))
    load_taps = pltpu.make_async_copy(taps_hbm, taps_ref, in_sems.at[CHUNKS])
    load_table = pltpu.make_async_copy(table_hbm, table, in_sems.at[CHUNKS + 1])
    load_taps.start()
    for load in load_volts:
        load.start()

    barrier = pltpu.get_barrier_semaphore()
    z_peers = [grid_device(x_hi, y, lax.rem(z + d, 8), block) for d in range(1, 8)]
    y_peers = [grid_device(x_hi, lax.rem(y + d, 4), z, block) for d in range(1, 4)]
    x_peers = [
        grid_device(lax.rem(x_hi + d // 4, 2), y, z, lax.rem(block + d % 4, 4)) for d in range(1, 8)
    ]
    for peer in x_peers + z_peers + y_peers:
        pl.semaphore_signal(barrier, inc=1, device_id=peer, device_id_type=MESH)

    load_table.start()

    def filter_frames(first, read):
        for part in range(FRAME // LANES):
            lane = part * LANES
            rows = [read(d, lane).astype(jnp.float32) for d in range(-(TAPS - 1), TAPS)]
            taps = [taps_ref[p : p + 1, lane : lane + LANES] for p in range(TAPS)]
            for t in range(TAPS):
                total = taps[0] * rows[t]
                for p in range(1, TAPS):
                    total = total + taps[p] * rows[t + p]
                for half in range(2):
                    filt32[part, pl.ds(half * frames + first + t, 8, stride=PITCH), :] = total[
                        half * 8 : half * 8 + 8
                    ]

    def read_volts(first):
        def read(d, lane):
            start = pl.multiple_of((first + d) * FRAME, FRAME) + lane
            return volts[:, pl.ds(start, LANES)]

        return read

    def filter_blocks(low, high):
        @pl.loop(low, high)
        def _(b):
            first = pl.multiple_of(b * TAPS, TAPS)
            filter_frames(first, read_volts(first))

    halo_copy = pltpu.make_async_remote_copy(
        src_ref=v_hbm.at[:, pl.ds(frames * FRAME - HALO, HALO)],
        dst_ref=halo,
        send_sem=halo_send,
        recv_sem=halo_recv,
        device_id=(lax.axis_index("inputs"), lax.rem(block + 1, blocks)),
        device_id_type=MESH,
    )

    pl.semaphore_wait(barrier, len(x_peers + y_peers + z_peers))

    @pl.when(block < blocks - 1)
    def _():
        halo_copy.start()

    for peer in y_peers:
        pl.semaphore_signal(y_sem, inc=1, device_id=peer, device_id_type=MESH)
    per = chunk // TAPS
    load_taps.wait()
    load_volts[0].wait()
    filter_blocks(1, per)
    for c in range(1, CHUNKS):
        load_volts[c].wait()
        filter_blocks(c * per, (c + 1) * per)
    pl.semaphore_wait(y_sem, len(y_peers))
    for peer in x_peers:
        pl.semaphore_signal(x_sem, inc=1, device_id=peer, device_id_type=MESH)

    def round_frames(low, high):
        for pair in range(inp // 2):
            for half in range(2):
                to, src = (2 * pair + half) * frames, pair * PITCH + half * frames
                for part in range(FRAME // LANES):
                    filt[to + low : to + high, part * LANES : (part + 1) * LANES] = filt32[
                        part, src + low : src + high, :
                    ].astype(jnp.bfloat16)

    round_frames(2 * TAPS, frames)

    @pl.when(block > 0)
    def _():
        halo_copy.wait_recv()

    @pl.when(block == 0)
    def _():
        halo[...] = jnp.zeros_like(halo)

    def read_first(d, lane):
        if d < 0:
            return halo[:, (d + TAPS - 1) * FRAME + lane : (d + TAPS - 1) * FRAME + lane + LANES]
        return volts[:, d * FRAME + lane : d * FRAME + lane + LANES]

    filter_frames(0, read_first)
    round_frames(0, 2 * TAPS)
    load_table.wait()

    low = lax.broadcasted_iota(jnp.int32, (8, LANES), 1) < LANES // 2

    me = lax.axis_index("inputs")
    span = groups * inp
    slot = pl.multiple_of(me * inp, inp)

    def transform(j):
        owner = lax.rem(block + j, blocks)
        rows = table[pl.ds(pl.multiple_of(owner * 2 * groups, 2 * groups), 2 * groups), :]
        for q in range(4):
            quarter = slice(q * 256, (q + 1) * 256)
            spec = lax.dot_general(
                rows,
                filt[quarter, :],
                (((1,), (1,)), ((), ())),
                preferred_element_type=jnp.float32,
            )
            for u in range(2):
                pair = 2 * q + u
                for g in range(groups // 8):
                    re = spec[g * 8 : g * 8 + 8, u * LANES : (u + 1) * LANES]
                    im = spec[groups + g * 8 : groups + g * 8 + 8, u * LANES : (u + 1) * LANES]
                    first = jnp.where(low, re, pltpu.roll(im, LANES // 2, 1))
                    second = jnp.where(low, pltpu.roll(re, LANES // 2, 1), im)
                    base = g * 8 * inp + pair
                    stage[pl.ds(base, 8, stride=inp), :] = first
                    stage[pl.ds(base + 8, 8, stride=inp), :] = second
        send[j * span : (j + 1) * span, :] = stage[...].astype(jnp.bfloat16)

    def copy_to(j, device, row):
        return pltpu.make_async_remote_copy(
            src_ref=send.at[pl.ds(pl.multiple_of(j * span + row * inp, inp), inp)],
            dst_ref=early.at[pl.ds(j * span + slot, inp)]
            if j < EARLY
            else late.at[j - EARLY, pl.ds(slot, inp)],
            send_sem=send_sem,
            recv_sem=recv_sems.at[0 if j < EARLY else 1],
            device_id=device,
            device_id_type=MESH,
        )

    def send_range(j, low_step, high_step, turn):
        @pl.loop(low_step, high_step)
        def _(s):
            tx = lax.rem(x_hi + s // 32 + turn * (s // 4), 2)
            ty = lax.rem(y + s // 8 + s, 4)
            tz = lax.rem(z + s, 8)
            row = tx * 32 + ty * 8 + tz
            copy_to(j, (row, lax.rem(block + j, blocks)), row).start()

    for j in range(blocks):
        transform(j)
        if j == 0:
            send_range(j, 1, groups // 2, 0)
            pl.semaphore_wait(x_sem, len(x_peers))
            send_range(j, groups // 2, groups, 0)
            early[pl.ds(slot, inp), :] = send[pl.ds(slot, inp), :]
        else:
            send_range(j, 0, groups, 1)

    @pl.when(block < blocks - 1)
    def _():
        halo_copy.wait_send()

    def arrivals(ref, sem):
        return pltpu.make_async_remote_copy(
            src_ref=ref,
            dst_ref=ref,
            send_sem=send_sem,
            recv_sem=recv_sems.at[sem],
            device_id=(me, lax.rem(block + 1, blocks)),
            device_id_type=MESH,
        )

    arrivals(early.at[0 : EARLY * span - inp], 0).wait_recv()

    def keep(place, c, prod):
        sums[place // (36 // PARTS)][place % (36 // PARTS), c] = prod

    tile_products(
        [early.at[j * span : (j + 1) * span] for j in range(EARLY)], keep, lambda *_: None
    )

    arrivals(send.at[0 : blocks * span - inp], 1).wait_send()
    arrivals(late, 1).wait_recv()


def tile_products(specs, keep, done):
    count_in, lanes = specs[0].shape
    nt = count_in // TILE
    left = jnp.concatenate([spec[...] for spec in specs], axis=-1)
    sign = jnp.where(lax.broadcasted_iota(jnp.int32, (1, lanes), 1) < lanes // 2, 1.0, -1.0)
    side = 2 * TILE
    for big in range(nt // 2):
        rows = slice(big * side, (big + 1) * side)
        twisted = jnp.concatenate(
            [
                (pltpu.roll(spec[rows, :].astype(jnp.float32), lanes // 2, 1) * sign).astype(
                    jnp.bfloat16
                )
                for spec in specs
            ],
            axis=-1,
        )
        both = jnp.concatenate([left[rows], twisted], axis=0)
        for cb in range(big, nt // 2):
            prod = lax.dot_general(
                both,
                left[cb * side : (cb + 1) * side],
                (((1,), (1,)), ((), ())),
                preferred_element_type=jnp.float32,
            )
            for a in range(2):
                row = 2 * big + a
                first = max(row, 2 * cb)
                place = row * nt - row * (row - 1) // 2 + first - row
                for col in range(first, 2 * cb + 2):
                    b = col - 2 * cb
                    for c in range(2):
                        lo = c * side + a * TILE
                        keep(
                            place + col - first,
                            c,
                            prod[lo : lo + TILE, b * TILE : (b + 1) * TILE],
                        )
                done(place, place + 2 * cb + 2 - first)


def channelize(voltages, pfb_taps, table):
    inp, samples = voltages.shape
    frames = samples // FRAME
    rows = inp * frames
    return pl.pallas_call(
        functools.partial(channel_kernel, frames),
        out_shape=[jax.ShapeDtypeStruct((4 - EARLY, 64 * inp, LANES), jnp.bfloat16)]
        + [jax.ShapeDtypeStruct((36 // PARTS, 2, TILE, TILE), jnp.float32)] * PARTS,
        in_specs=[
            pl.BlockSpec(memory_space=pltpu.HBM),
            pl.BlockSpec(memory_space=pltpu.HBM),
            pl.BlockSpec(memory_space=pltpu.HBM),
        ],
        out_specs=[pl.BlockSpec(memory_space=pltpu.VMEM)] * (1 + PARTS),
        scratch_shapes=[
            pltpu.VMEM((inp, samples), jnp.bfloat16),
            pltpu.VMEM((TAPS, FRAME), jnp.float32),
            pltpu.VMEM((2 * F, FRAME), jnp.bfloat16),
            pltpu.VMEM((inp, HALO), jnp.bfloat16),
            pltpu.VMEM((FRAME // LANES, 8 * PITCH, LANES), jnp.float32),
            pltpu.VMEM((rows, FRAME), jnp.bfloat16),
            pltpu.VMEM((64 * inp, LANES), jnp.float32),
            pltpu.VMEM((4 * 64 * inp, LANES), jnp.bfloat16),
            pltpu.VMEM((EARLY * 64 * inp, LANES), jnp.bfloat16),
            pltpu.SemaphoreType.DMA((CHUNKS + 2,)),
            pltpu.SemaphoreType.DMA,
            pltpu.SemaphoreType.DMA,
            pltpu.SemaphoreType.DMA,
            pltpu.SemaphoreType.DMA((2,)),
            pltpu.SemaphoreType.REGULAR,
            pltpu.SemaphoreType.REGULAR,
        ],
        compiler_params=pltpu.CompilerParams(
            collective_id=0, has_side_effects=True, vmem_limit_bytes=VMEM_BYTES
        ),
    )(voltages, pfb_taps, table)


def tile_kernel(scale, late, *refs):
    sums = refs[:PARTS]
    out_hbm, tiles, sem = refs[PARTS:]
    copies = []

    def keep(place, c, prod):
        earlier = sums[place // (36 // PARTS)][place % (36 // PARTS), c]
        tiles[place, c] = (earlier + prod) * scale

    def done(low, high):
        copy = pltpu.make_async_copy(
            tiles.at[low:high], out_hbm.at[0, low:high], sem.at[len(copies)]
        )
        copy.start()
        copies.append(copy)

    tile_products([late.at[j] for j in range(late.shape[0])], keep, done)
    for copy in copies:
        copy.wait()


def tile_sums(late, sums, scale):
    nt = late.shape[1] // TILE
    pairs = nt * (nt + 1) // 2
    return pl.pallas_call(
        functools.partial(tile_kernel, scale),
        out_shape=jax.ShapeDtypeStruct((1, pairs, 2, TILE, TILE), jnp.float32),
        in_specs=[pl.BlockSpec(memory_space=pltpu.VMEM)] * (1 + PARTS),
        out_specs=pl.BlockSpec(memory_space=pl.ANY),
        scratch_shapes=[
            pltpu.VMEM((pairs, 2, TILE, TILE), jnp.float32),
            pltpu.SemaphoreType.DMA((nt // 2 * (nt // 2 + 1),)),
        ],
        compiler_params=pltpu.CompilerParams(vmem_limit_bytes=32 << 20),
    )(late, *sums)


def on_device(voltages, pfb_taps):
    table = jnp.asarray(dft_table(F, FRAME, lax.axis_size("tm")))
    frames = voltages.shape[1] // FRAME
    args = [pltpu.with_memory_space_constraint(a, pltpu.HBM) for a in (voltages, pfb_taps, table)]
    late, *sums = channelize(*args)
    return tile_sums(late, sums, 1.0 / (frames * lax.axis_size("tm")))


def solution(mesh):
    in_specs = (P("inputs", "tm"), P())
    out_specs = P(("inputs", "tm"), None, None, None, None)
    return jax.shard_map(
        on_device, mesh=mesh, in_specs=in_specs, out_specs=out_specs, check_vma=False
    )
```

```python
import functools

import jax
import jax.numpy as jnp
import numpy as np
from jax import lax
from jax.experimental import pallas as pl
from jax.experimental.pallas import tpu as pltpu
from jax.sharding import PartitionSpec as P

F = 256
TAPS = 8
TILE = 128
FRAME = 512
HALO = (TAPS - 1) * FRAME
LANES = 128
CHUNKS = 4
EARLY = 3
PITCH = 136
PARTS = 6
VMEM_BYTES = 40 << 20
MESH = pl.DeviceIdType.MESH


def dft_table(chans, length, owners):
    freq = np.arange(chans, dtype=np.int32)
    samp = np.arange(length, dtype=np.int32)
    phase = (freq[:, None] * samp[None, :]) % length
    angle = 2.0 * np.pi / length * phase.astype(np.float64)
    vals = np.stack([np.cos(angle), -np.sin(angle)]) / length**0.5
    vals = vals.reshape(2, chans // owners, owners, length).transpose(2, 0, 1, 3)
    vals = vals.reshape(2 * chans, length).astype(np.float32).astype(jnp.bfloat16)
    return vals


def grid_coords():
    along = lax.axis_index("inputs")
    block = lax.axis_index("tm")
    return along // 32, (along // 8) % 4, along % 8, block


def grid_device(x_hi, y, z, block):
    return (x_hi * 32 + y * 8 + z, block)


def channel_kernel(
    frames, v_hbm, taps_hbm, table_hbm, late, *refs
):
    sums = refs[:PARTS]
    (
        volts, taps_ref, table, halo, filt32, filt, stage, send, early,
        in_sems, halo_send, halo_recv, send_sem, recv_sems, y_sem, x_sem,
    ) = refs[PARTS:]
    x_hi, y, z, block = grid_coords()
    blocks = 4
    groups = 64
    inp = v_hbm.shape[0]

    chunk = frames // CHUNKS
    load_volts = []
    for c in range(CHUNKS):
        part = pl.ds(c * chunk * FRAME, chunk * FRAME)
        load_volts.append(pltpu.make_async_copy(v_hbm.at[:, part], volts.at[:, part], in_sems.at[c]))
    load_taps = pltpu.make_async_copy(taps_hbm, taps_ref, in_sems.at[CHUNKS])
    load_table = pltpu.make_async_copy(table_hbm, table, in_sems.at[CHUNKS + 1])
    barrier = pltpu.get_barrier_semaphore()
    z_peers = [grid_device(x_hi, y, lax.rem(z + d, 8), block) for d in range(1, 8)]
    y_peers = [grid_device(x_hi, lax.rem(y + d, 4), z, block) for d in range(1, 4)]
    x_peers = [
        grid_device(lax.rem(x_hi + d // 4, 2), y, z, lax.rem(block + d % 4, 4)) for d in range(1, 8)
    ]
    for peer in x_peers + z_peers + y_peers:
        pl.semaphore_signal(barrier, inc=1, device_id=peer, device_id_type=MESH)
    load_taps.start()
    for load in load_volts:
        load.start()

    load_table.start()

    def filter_frames(first, read):
        for part in range(FRAME // LANES):
            lane = part * LANES
            rows = [read(d, lane).astype(jnp.float32) for d in range(-(TAPS - 1), TAPS)]
            taps = [taps_ref[p : p + 1, lane : lane + LANES] for p in range(TAPS)]
            for t in range(TAPS):
                total = taps[0] * rows[t]
                for p in range(1, TAPS):
                    total = total + taps[p] * rows[t + p]
                for half in range(2):
                    filt32[part, pl.ds(half * frames + first + t, 8, stride=PITCH), :] = total[
                        half * 8 : half * 8 + 8
                    ]

    def read_volts(first):
        def read(d, lane):
            start = pl.multiple_of((first + d) * FRAME, FRAME) + lane
            return volts[:, pl.ds(start, LANES)]

        return read

    def filter_blocks(low, high):
        @pl.loop(low, high)
        def _(b):
            first = pl.multiple_of(b * TAPS, TAPS)
            filter_frames(first, read_volts(first))

    halo_copy = pltpu.make_async_remote_copy(
        src_ref=v_hbm.at[:, pl.ds(frames * FRAME - HALO, HALO)],
        dst_ref=halo,
        send_sem=halo_send,
        recv_sem=halo_recv,
        device_id=(lax.axis_index("inputs"), lax.rem(block + 1, blocks)),
        device_id_type=MESH,
    )

    pl.semaphore_wait(barrier, len(x_peers + y_peers + z_peers))

    @pl.when(block < blocks - 1)
    def _():
        halo_copy.start()

    for peer in y_peers:
        pl.semaphore_signal(y_sem, inc=1, device_id=peer, device_id_type=MESH)
    per = chunk // TAPS
    load_taps.wait()
    load_volts[0].wait()
    filter_blocks(1, per)
    for c in range(1, CHUNKS):
        load_volts[c].wait()
        filter_blocks(c * per, (c + 1) * per)
    pl.semaphore_wait(y_sem, len(y_peers))
    for peer in x_peers:
        pl.semaphore_signal(x_sem, inc=1, device_id=peer, device_id_type=MESH)

    def round_frames(low, high):
        for pair in range(inp // 2):
            for half in range(2):
                to, src = (2 * pair + half) * frames, pair * PITCH + half * frames
                for part in range(FRAME // LANES):
                    filt[to + low : to + high, part * LANES : (part + 1) * LANES] = filt32[
                        part, src + low : src + high, :
                    ].astype(jnp.bfloat16)

    round_frames(2 * TAPS, frames)

    @pl.when(block > 0)
    def _():
        halo_copy.wait_recv()

    @pl.when(block == 0)
    def _():
        halo[...] = jnp.zeros_like(halo)

    def read_first(d, lane):
        if d < 0:
            return halo[:, (d + TAPS - 1) * FRAME + lane : (d + TAPS - 1) * FRAME + lane + LANES]
        return volts[:, d * FRAME + lane : d * FRAME + lane + LANES]

    filter_frames(0, read_first)
    round_frames(0, 2 * TAPS)
    load_table.wait()

    low = lax.broadcasted_iota(jnp.int32, (8, LANES), 1) < LANES // 2

    me = lax.axis_index("inputs")
    span = groups * inp
    slot = pl.multiple_of(me * inp, inp)

    def transform(j):
        owner = lax.rem(block + j, blocks)
        rows = table[pl.ds(pl.multiple_of(owner * 2 * groups, 2 * groups), 2 * groups), :]
        for q in range(4):
            quarter = slice(q * 256, (q + 1) * 256)
            spec = lax.dot_general(
                rows,
                filt[quarter, :],
                (((1,), (1,)), ((), ())),
                preferred_element_type=jnp.float32,
            )
            for u in range(2):
                pair = 2 * q + u
                for g in range(groups // 8):
                    re = spec[g * 8 : g * 8 + 8, u * LANES : (u + 1) * LANES]
                    im = spec[groups + g * 8 : groups + g * 8 + 8, u * LANES : (u + 1) * LANES]
                    first = jnp.where(low, re, pltpu.roll(im, LANES // 2, 1))
                    second = jnp.where(low, pltpu.roll(re, LANES // 2, 1), im)
                    base = g * 8 * inp + pair
                    stage[pl.ds(base, 8, stride=inp), :] = first
                    stage[pl.ds(base + 8, 8, stride=inp), :] = second
        send[j * span : (j + 1) * span, :] = stage[...].astype(jnp.bfloat16)

    def copy_to(j, device, row):
        return pltpu.make_async_remote_copy(
            src_ref=send.at[pl.ds(pl.multiple_of(j * span + row * inp, inp), inp)],
            dst_ref=early.at[pl.ds(j * span + slot, inp)]
            if j < EARLY
            else late.at[j - EARLY, pl.ds(slot, inp)],
            send_sem=send_sem,
            recv_sem=recv_sems.at[0 if j < EARLY else 1],
            device_id=device,
            device_id_type=MESH,
        )

    def send_range(j, low_step, high_step, turn):
        @pl.loop(low_step, high_step)
        def _(s):
            tx = lax.rem(x_hi + s // 32 + turn * (s // 4), 2)
            ty = lax.rem(y + s // 8 + s, 4)
            tz = lax.rem(z + s, 8)
            row = tx * 32 + ty * 8 + tz
            copy_to(j, (row, lax.rem(block + j, blocks)), row).start()

    for j in range(blocks):
        transform(j)
        if j == 0:
            send_range(j, 1, groups // 2, 0)
            pl.semaphore_wait(x_sem, len(x_peers))
            send_range(j, groups // 2, groups, 0)
            early[pl.ds(slot, inp), :] = send[pl.ds(slot, inp), :]
        else:
            send_range(j, 0, groups, 1)

    @pl.when(block < blocks - 1)
    def _():
        halo_copy.wait_send()

    def arrivals(ref, sem):
        return pltpu.make_async_remote_copy(
            src_ref=ref,
            dst_ref=ref,
            send_sem=send_sem,
            recv_sem=recv_sems.at[sem],
            device_id=(me, lax.rem(block + 1, blocks)),
            device_id_type=MESH,
        )

    arrivals(early.at[0 : EARLY * span - inp], 0).wait_recv()

    def keep(place, c, prod):
        sums[place // (36 // PARTS)][place % (36 // PARTS), c] = prod

    tile_products(
        [early.at[j * span : (j + 1) * span] for j in range(EARLY)], keep, lambda *_: None
    )

    arrivals(send.at[0 : blocks * span - inp], 1).wait_send()
    arrivals(late, 1).wait_recv()


def tile_products(specs, keep, done):
    count_in, lanes = specs[0].shape
    nt = count_in // TILE
    left = jnp.concatenate([spec[...] for spec in specs], axis=-1)
    sign = jnp.where(lax.broadcasted_iota(jnp.int32, (1, lanes), 1) < lanes // 2, 1.0, -1.0)
    side = 2 * TILE
    for big in range(nt // 2):
        rows = slice(big * side, (big + 1) * side)
        twisted = jnp.concatenate(
            [
                (pltpu.roll(spec[rows, :].astype(jnp.float32), lanes // 2, 1) * sign).astype(
                    jnp.bfloat16
                )
                for spec in specs
            ],
            axis=-1,
        )
        both = jnp.concatenate([left[rows], twisted], axis=0)
        for cb in range(big, nt // 2):
            prod = lax.dot_general(
                both,
                left[cb * side : (cb + 1) * side],
                (((1,), (1,)), ((), ())),
                preferred_element_type=jnp.float32,
            )
            for a in range(2):
                row = 2 * big + a
                first = max(row, 2 * cb)
                place = row * nt - row * (row - 1) // 2 + first - row
                for col in range(first, 2 * cb + 2):
                    b = col - 2 * cb
                    for c in range(2):
                        lo = c * side + a * TILE
                        keep(
                            place + col - first,
                            c,
                            prod[lo : lo + TILE, b * TILE : (b + 1) * TILE],
                        )
                done(place, place + 2 * cb + 2 - first)


def channelize(voltages, pfb_taps, table):
    inp, samples = voltages.shape
    frames = samples // FRAME
    rows = inp * frames
    return pl.pallas_call(
        functools.partial(channel_kernel, frames),
        out_shape=[jax.ShapeDtypeStruct((4 - EARLY, 64 * inp, LANES), jnp.bfloat16)]
        + [jax.ShapeDtypeStruct((36 // PARTS, 2, TILE, TILE), jnp.float32)] * PARTS,
        in_specs=[
            pl.BlockSpec(memory_space=pltpu.HBM),
            pl.BlockSpec(memory_space=pltpu.HBM),
            pl.BlockSpec(memory_space=pltpu.HBM),
        ],
        out_specs=[pl.BlockSpec(memory_space=pltpu.VMEM)] * (1 + PARTS),
        scratch_shapes=[
            pltpu.VMEM((inp, samples), jnp.bfloat16),
            pltpu.VMEM((TAPS, FRAME), jnp.float32),
            pltpu.VMEM((2 * F, FRAME), jnp.bfloat16),
            pltpu.VMEM((inp, HALO), jnp.bfloat16),
            pltpu.VMEM((FRAME // LANES, 8 * PITCH, LANES), jnp.float32),
            pltpu.VMEM((rows, FRAME), jnp.bfloat16),
            pltpu.VMEM((64 * inp, LANES), jnp.float32),
            pltpu.VMEM((4 * 64 * inp, LANES), jnp.bfloat16),
            pltpu.VMEM((EARLY * 64 * inp, LANES), jnp.bfloat16),
            pltpu.SemaphoreType.DMA((CHUNKS + 2,)),
            pltpu.SemaphoreType.DMA,
            pltpu.SemaphoreType.DMA,
            pltpu.SemaphoreType.DMA,
            pltpu.SemaphoreType.DMA((2,)),
            pltpu.SemaphoreType.REGULAR,
            pltpu.SemaphoreType.REGULAR,
        ],
        compiler_params=pltpu.CompilerParams(
            collective_id=0, has_side_effects=True, vmem_limit_bytes=VMEM_BYTES
        ),
    )(voltages, pfb_taps, table)


def tile_kernel(scale, late, *refs):
    sums = refs[:PARTS]
    out_hbm, tiles, sem = refs[PARTS:]
    copies = []

    def keep(place, c, prod):
        earlier = sums[place // (36 // PARTS)][place % (36 // PARTS), c]
        tiles[place, c] = (earlier + prod) * scale

    def done(low, high):
        copy = pltpu.make_async_copy(
            tiles.at[low:high], out_hbm.at[0, low:high], sem.at[len(copies)]
        )
        copy.start()
        copies.append(copy)

    tile_products([late.at[j] for j in range(late.shape[0])], keep, done)
    for copy in copies:
        copy.wait()


def tile_sums(late, sums, scale):
    nt = late.shape[1] // TILE
    pairs = nt * (nt + 1) // 2
    return pl.pallas_call(
        functools.partial(tile_kernel, scale),
        out_shape=jax.ShapeDtypeStruct((1, pairs, 2, TILE, TILE), jnp.float32),
        in_specs=[pl.BlockSpec(memory_space=pltpu.VMEM)] * (1 + PARTS),
        out_specs=pl.BlockSpec(memory_space=pl.ANY),
        scratch_shapes=[
            pltpu.VMEM((pairs, 2, TILE, TILE), jnp.float32),
            pltpu.SemaphoreType.DMA((nt // 2 * (nt // 2 + 1),)),
        ],
        compiler_params=pltpu.CompilerParams(vmem_limit_bytes=32 << 20),
    )(late, *sums)


def on_device(voltages, pfb_taps):
    table = jnp.asarray(dft_table(F, FRAME, lax.axis_size("tm")))
    frames = voltages.shape[1] // FRAME
    args = [pltpu.with_memory_space_constraint(a, pltpu.HBM) for a in (voltages, pfb_taps, table)]
    late, *sums = channelize(*args)
    return tile_sums(late, sums, 1.0 / (frames * lax.axis_size("tm")))


def solution(mesh):
    in_specs = (P("inputs", "tm"), P())
    out_specs = P(("inputs", "tm"), None, None, None, None)
    return jax.shard_map(
        on_device, mesh=mesh, in_specs=in_specs, out_specs=out_specs, check_vma=False
    )
```

```python
import functools

import jax
import jax.numpy as jnp
import numpy as np
from jax import lax
from jax.experimental import pallas as pl
from jax.experimental.pallas import tpu as pltpu
from jax.sharding import PartitionSpec as P

F = 256
TAPS = 8
TILE = 128
FRAME = 512
HALO = (TAPS - 1) * FRAME
LANES = 128
CHUNKS = 4
EARLY = 3
PITCH = 136
PARTS = 6
VMEM_BYTES = 40 << 20
MESH = pl.DeviceIdType.MESH


def dft_table(chans, length, owners):
    freq = np.arange(chans, dtype=np.int32)
    samp = np.arange(length, dtype=np.int32)
    phase = (freq[:, None] * samp[None, :]) % length
    angle = 2.0 * np.pi / length * phase.astype(np.float64)
    vals = np.stack([np.cos(angle), -np.sin(angle)]) / length**0.5
    vals = vals.reshape(2, chans // owners, owners, length).transpose(2, 0, 1, 3)
    vals = vals.reshape(2 * chans, length).astype(np.float32).astype(jnp.bfloat16)
    return vals


def grid_coords():
    along = lax.axis_index("inputs")
    block = lax.axis_index("tm")
    return along // 32, (along // 8) % 4, along % 8, block


def grid_device(x_hi, y, z, block):
    return (x_hi * 32 + y * 8 + z, block)


def channel_kernel(
    frames, v_hbm, taps_hbm, table_hbm, late, *refs
):
    sums = refs[:PARTS]
    (
        volts, taps_ref, table, halo, filt32, filt, stage, send, early,
        in_sems, halo_send, halo_recv, send_sem, recv_sems, y_sem, x_sem,
    ) = refs[PARTS:]
    x_hi, y, z, block = grid_coords()
    blocks = 4
    groups = 64
    inp = v_hbm.shape[0]

    chunk = frames // CHUNKS
    load_volts = []
    for c in range(CHUNKS):
        part = pl.ds(c * chunk * FRAME, chunk * FRAME)
        load_volts.append(pltpu.make_async_copy(v_hbm.at[:, part], volts.at[:, part], in_sems.at[c]))
    load_taps = pltpu.make_async_copy(taps_hbm, taps_ref, in_sems.at[CHUNKS])
    load_table = pltpu.make_async_copy(table_hbm, table, in_sems.at[CHUNKS + 1])
    barrier = pltpu.get_barrier_semaphore()
    z_peers = [grid_device(x_hi, y, lax.rem(z + d, 8), block) for d in range(1, 8)]
    y_peers = [grid_device(x_hi, lax.rem(y + d, 4), z, block) for d in range(1, 4)]
    x_peers = [
        grid_device(lax.rem(x_hi + d // 4, 2), y, z, lax.rem(block + d % 4, 4)) for d in range(1, 8)
    ]
    for peer in x_peers + z_peers + y_peers:
        pl.semaphore_signal(barrier, inc=1, device_id=peer, device_id_type=MESH)
    load_taps.start()
    for load in load_volts:
        load.start()

    load_table.start()

    def filter_frames(first, read):
        for part in range(FRAME // LANES):
            lane = part * LANES
            rows = [read(d, lane).astype(jnp.float32) for d in range(-(TAPS - 1), TAPS)]
            taps = [taps_ref[p : p + 1, lane : lane + LANES] for p in range(TAPS)]
            for t in range(TAPS):
                total = taps[0] * rows[t]
                for p in range(1, TAPS):
                    total = total + taps[p] * rows[t + p]
                for half in range(2):
                    filt32[part, pl.ds(half * frames + first + t, 8, stride=PITCH), :] = total[
                        half * 8 : half * 8 + 8
                    ]

    def read_volts(first):
        def read(d, lane):
            start = pl.multiple_of((first + d) * FRAME, FRAME) + lane
            return volts[:, pl.ds(start, LANES)]

        return read

    def filter_blocks(low, high):
        @pl.loop(low, high)
        def _(b):
            first = pl.multiple_of(b * TAPS, TAPS)
            filter_frames(first, read_volts(first))

    halo_copy = pltpu.make_async_remote_copy(
        src_ref=v_hbm.at[:, pl.ds(frames * FRAME - HALO, HALO)],
        dst_ref=halo,
        send_sem=halo_send,
        recv_sem=halo_recv,
        device_id=(lax.axis_index("inputs"), lax.rem(block + 1, blocks)),
        device_id_type=MESH,
    )

    pl.semaphore_wait(barrier, len(x_peers + y_peers + z_peers))

    @pl.when(block < blocks - 1)
    def _():
        halo_copy.start()

    for peer in y_peers:
        pl.semaphore_signal(y_sem, inc=1, device_id=peer, device_id_type=MESH)
    per = chunk // TAPS
    load_taps.wait()
    load_volts[0].wait()
    filter_blocks(1, per)
    for c in range(1, CHUNKS):
        load_volts[c].wait()
        filter_blocks(c * per, (c + 1) * per)
    pl.semaphore_wait(y_sem, len(y_peers))
    for peer in x_peers:
        pl.semaphore_signal(x_sem, inc=1, device_id=peer, device_id_type=MESH)

    def round_frames(low, high):
        for pair in range(inp // 2):
            for half in range(2):
                to, src = (2 * pair + half) * frames, pair * PITCH + half * frames
                for part in range(FRAME // LANES):
                    filt[to + low : to + high, part * LANES : (part + 1) * LANES] = filt32[
                        part, src + low : src + high, :
                    ].astype(jnp.bfloat16)

    round_frames(2 * TAPS, frames)

    @pl.when(block > 0)
    def _():
        halo_copy.wait_recv()

    @pl.when(block == 0)
    def _():
        halo[...] = jnp.zeros_like(halo)

    def read_first(d, lane):
        if d < 0:
            return halo[:, (d + TAPS - 1) * FRAME + lane : (d + TAPS - 1) * FRAME + lane + LANES]
        return volts[:, d * FRAME + lane : d * FRAME + lane + LANES]

    filter_frames(0, read_first)
    round_frames(0, 2 * TAPS)
    load_table.wait()

    low = lax.broadcasted_iota(jnp.int32, (8, LANES), 1) < LANES // 2

    me = lax.axis_index("inputs")
    span = groups * inp
    slot = pl.multiple_of(me * inp, inp)

    def transform(j):
        owner = lax.rem(block + j, blocks)
        rows = table[pl.ds(pl.multiple_of(owner * 2 * groups, 2 * groups), 2 * groups), :]
        for q in range(4):
            quarter = slice(q * 256, (q + 1) * 256)
            spec = lax.dot_general(
                rows,
                filt[quarter, :],
                (((1,), (1,)), ((), ())),
                preferred_element_type=jnp.float32,
            )
            for u in range(2):
                pair = 2 * q + u
                for g in range(groups // 8):
                    re = spec[g * 8 : g * 8 + 8, u * LANES : (u + 1) * LANES]
                    im = spec[groups + g * 8 : groups + g * 8 + 8, u * LANES : (u + 1) * LANES]
                    first = jnp.where(low, re, pltpu.roll(im, LANES // 2, 1))
                    second = jnp.where(low, pltpu.roll(re, LANES // 2, 1), im)
                    base = g * 8 * inp + pair
                    stage[pl.ds(base, 8, stride=inp), :] = first
                    stage[pl.ds(base + 8, 8, stride=inp), :] = second
        send[j * span : (j + 1) * span, :] = stage[0:span, :].astype(jnp.bfloat16)

    def copy_to(j, device, row):
        return pltpu.make_async_remote_copy(
            src_ref=send.at[pl.ds(pl.multiple_of(j * span + row * inp, inp), inp)],
            dst_ref=early.at[pl.ds(j * span + slot, inp)]
            if j < EARLY
            else late.at[j - EARLY, pl.ds(slot, inp)],
            send_sem=send_sem,
            recv_sem=recv_sems.at[0 if j < EARLY else 1],
            device_id=device,
            device_id_type=MESH,
        )

    def send_range(j, low_step, high_step, turn):
        @pl.loop(low_step, high_step)
        def _(s):
            tx = lax.rem(x_hi + s // 32 + turn * (s // 4), 2)
            ty = lax.rem(y + s // 8 + s, 4)
            tz = lax.rem(z + s, 8)
            row = tx * 32 + ty * 8 + tz
            copy_to(j, (row, lax.rem(block + j, blocks)), row).start()

    for j in range(blocks):
        transform(j)
        if j == 0:
            send_range(j, 1, groups // 2, 0)
            pl.semaphore_wait(x_sem, len(x_peers))
            send_range(j, groups // 2, groups, 0)
            early[pl.ds(slot, inp), :] = send[pl.ds(slot, inp), :]
        else:
            send_range(j, 0, groups, 1)

    @pl.when(block < blocks - 1)
    def _():
        halo_copy.wait_send()

    def arrivals(ref, sem):
        return pltpu.make_async_remote_copy(
            src_ref=ref,
            dst_ref=ref,
            send_sem=send_sem,
            recv_sem=recv_sems.at[sem],
            device_id=(me, lax.rem(block + 1, blocks)),
            device_id_type=MESH,
        )

    arrivals(early.at[0 : EARLY * span - inp], 0).wait_recv()

    def keep(place, c, prod):
        sums[place // (36 // PARTS)][place % (36 // PARTS), c] = prod

    tile_products(
        [early.at[j * span : (j + 1) * span] for j in range(EARLY)], keep, lambda *_: None
    )

    arrivals(send.at[0 : blocks * span - inp], 1).wait_send()
    arrivals(late, 1).wait_recv()


def tile_products(specs, keep, done):
    count_in, lanes = specs[0].shape
    nt = count_in // TILE
    left = jnp.concatenate([spec[...] for spec in specs], axis=-1)
    sign = jnp.where(lax.broadcasted_iota(jnp.int32, (1, lanes), 1) < lanes // 2, 1.0, -1.0)
    side = 2 * TILE
    for big in range(nt // 2):
        rows = slice(big * side, (big + 1) * side)
        twisted = jnp.concatenate(
            [
                (pltpu.roll(spec[rows, :].astype(jnp.float32), lanes // 2, 1) * sign).astype(
                    jnp.bfloat16
                )
                for spec in specs
            ],
            axis=-1,
        )
        both = jnp.concatenate([left[rows], twisted], axis=0)
        for cb in range(big, nt // 2):
            prod = lax.dot_general(
                both,
                left[cb * side : (cb + 1) * side],
                (((1,), (1,)), ((), ())),
                preferred_element_type=jnp.float32,
            )
            for a in range(2):
                row = 2 * big + a
                first = max(row, 2 * cb)
                place = row * nt - row * (row - 1) // 2 + first - row
                for col in range(first, 2 * cb + 2):
                    b = col - 2 * cb
                    for c in range(2):
                        lo = c * side + a * TILE
                        keep(
                            place + col - first,
                            c,
                            prod[lo : lo + TILE, b * TILE : (b + 1) * TILE],
                        )
                done(place, place + 2 * cb + 2 - first)


def channelize(voltages, pfb_taps, table):
    inp, samples = voltages.shape
    frames = samples // FRAME
    rows = inp * frames
    return pl.pallas_call(
        functools.partial(channel_kernel, frames),
        out_shape=[jax.ShapeDtypeStruct((4 - EARLY, 64 * inp, LANES), jnp.bfloat16)]
        + [jax.ShapeDtypeStruct((36 // PARTS, 2, TILE, TILE), jnp.float32)] * PARTS,
        in_specs=[
            pl.BlockSpec(memory_space=pltpu.HBM),
            pl.BlockSpec(memory_space=pltpu.HBM),
            pl.BlockSpec(memory_space=pltpu.HBM),
        ],
        out_specs=[pl.BlockSpec(memory_space=pltpu.VMEM)] * (1 + PARTS),
        scratch_shapes=[
            pltpu.VMEM((inp, samples), jnp.bfloat16),
            pltpu.VMEM((TAPS, FRAME), jnp.float32),
            pltpu.VMEM((2 * F, FRAME), jnp.bfloat16),
            pltpu.VMEM((inp, HALO), jnp.bfloat16),
            pltpu.VMEM((FRAME // LANES, 8 * PITCH + 2 * frames, LANES), jnp.float32),
            pltpu.VMEM((rows, FRAME), jnp.bfloat16),
            pltpu.VMEM((64 * inp + inp, LANES), jnp.float32),
            pltpu.VMEM((4 * 64 * inp, LANES), jnp.bfloat16),
            pltpu.VMEM((EARLY * 64 * inp, LANES), jnp.bfloat16),
            pltpu.SemaphoreType.DMA((CHUNKS + 2,)),
            pltpu.SemaphoreType.DMA,
            pltpu.SemaphoreType.DMA,
            pltpu.SemaphoreType.DMA,
            pltpu.SemaphoreType.DMA((2,)),
            pltpu.SemaphoreType.REGULAR,
            pltpu.SemaphoreType.REGULAR,
        ],
        compiler_params=pltpu.CompilerParams(
            collective_id=0, has_side_effects=True, vmem_limit_bytes=VMEM_BYTES
        ),
    )(voltages, pfb_taps, table)


def tile_kernel(scale, late, *refs):
    sums = refs[:PARTS]
    out_hbm, tiles, sem = refs[PARTS:]
    copies = []

    def keep(place, c, prod):
        earlier = sums[place // (36 // PARTS)][place % (36 // PARTS), c]
        tiles[place, c] = (earlier + prod) * scale

    def done(low, high):
        copy = pltpu.make_async_copy(
            tiles.at[low:high], out_hbm.at[0, low:high], sem.at[len(copies)]
        )
        copy.start()
        copies.append(copy)

    tile_products([late.at[j] for j in range(late.shape[0])], keep, done)
    for copy in copies:
        copy.wait()


def tile_sums(late, sums, scale):
    nt = late.shape[1] // TILE
    pairs = nt * (nt + 1) // 2
    return pl.pallas_call(
        functools.partial(tile_kernel, scale),
        out_shape=jax.ShapeDtypeStruct((1, pairs, 2, TILE, TILE), jnp.float32),
        in_specs=[pl.BlockSpec(memory_space=pltpu.VMEM)] * (1 + PARTS),
        out_specs=pl.BlockSpec(memory_space=pl.ANY),
        scratch_shapes=[
            pltpu.VMEM((pairs, 2, TILE, TILE), jnp.float32),
            pltpu.SemaphoreType.DMA((nt // 2 * (nt // 2 + 1),)),
        ],
        compiler_params=pltpu.CompilerParams(vmem_limit_bytes=32 << 20),
    )(late, *sums)


def on_device(voltages, pfb_taps):
    table = jnp.asarray(dft_table(F, FRAME, lax.axis_size("tm")))
    frames = voltages.shape[1] // FRAME
    args = [pltpu.with_memory_space_constraint(a, pltpu.HBM) for a in (voltages, pfb_taps, table)]
    late, *sums = channelize(*args)
    return tile_sums(late, sums, 1.0 / (frames * lax.axis_size("tm")))


def solution(mesh):
    in_specs = (P("inputs", "tm"), P())
    out_specs = P(("inputs", "tm"), None, None, None, None)
    return jax.shard_map(
        on_device, mesh=mesh, in_specs=in_specs, out_specs=out_specs, check_vma=False
    )
```

```python
import functools

import jax
import jax.numpy as jnp
import numpy as np
from jax import lax
from jax.experimental import pallas as pl
from jax.experimental.pallas import tpu as pltpu
from jax.sharding import PartitionSpec as P

F = 256
TAPS = 8
TILE = 128
FRAME = 512
HALO = (TAPS - 1) * FRAME
LANES = 128
CHUNKS = 4
EARLY = 3
PITCH = 136
PARTS = 6
VMEM_BYTES = 40 << 20
MESH = pl.DeviceIdType.MESH


def dft_table(chans, length, owners):
    freq = np.arange(chans, dtype=np.int32)
    samp = np.arange(length, dtype=np.int32)
    phase = (freq[:, None] * samp[None, :]) % length
    angle = 2.0 * np.pi / length * phase.astype(np.float64)
    vals = np.stack([np.cos(angle), -np.sin(angle)]) / length**0.5
    vals = vals.reshape(2, chans // owners, owners, length).transpose(2, 0, 1, 3)
    vals = vals.reshape(2 * chans, length).astype(np.float32).astype(jnp.bfloat16)
    return vals


def grid_coords():
    along = lax.axis_index("inputs")
    block = lax.axis_index("tm")
    return along // 32, (along // 8) % 4, along % 8, block


def grid_device(x_hi, y, z, block):
    return (x_hi * 32 + y * 8 + z, block)


def channel_kernel(
    frames, v_hbm, taps_hbm, table_hbm, late, *refs
):
    sums = refs[:PARTS]
    (
        volts, taps_ref, table, halo, filt32, filt, stage, send, early,
        in_sems, halo_send, halo_recv, send_sem, recv_sems, y_sem, x_sem,
    ) = refs[PARTS:]
    x_hi, y, z, block = grid_coords()
    blocks = 4
    groups = 64
    inp = v_hbm.shape[0]

    chunk = frames // CHUNKS
    load_volts = []
    for c in range(CHUNKS):
        part = pl.ds(c * chunk * FRAME, chunk * FRAME)
        load_volts.append(pltpu.make_async_copy(v_hbm.at[:, part], volts.at[:, part], in_sems.at[c]))
    load_taps = pltpu.make_async_copy(taps_hbm, taps_ref, in_sems.at[CHUNKS])
    load_table = pltpu.make_async_copy(table_hbm, table, in_sems.at[CHUNKS + 1])
    barrier = pltpu.get_barrier_semaphore()
    z_peers = [grid_device(x_hi, y, lax.rem(z + d, 8), block) for d in range(1, 8)]
    y_peers = [grid_device(x_hi, lax.rem(y + d, 4), z, block) for d in range(1, 4)]
    x_peers = [
        grid_device(lax.rem(x_hi + d // 4, 2), y, z, lax.rem(block + d % 4, 4)) for d in range(1, 8)
    ]
    for peer in x_peers + z_peers + y_peers:
        pl.semaphore_signal(barrier, inc=1, device_id=peer, device_id_type=MESH)
    load_taps.start()
    for load in load_volts:
        load.start()

    load_table.start()

    def filter_frames(first, read):
        for part in range(FRAME // LANES):
            lane = part * LANES
            rows = [read(d, lane).astype(jnp.float32) for d in range(-(TAPS - 1), TAPS)]
            taps = [taps_ref[p : p + 1, lane : lane + LANES] for p in range(TAPS)]
            for t in range(TAPS):
                total = taps[0] * rows[t]
                for p in range(1, TAPS):
                    total = total + taps[p] * rows[t + p]
                for half in range(2):
                    filt32[part, pl.ds(half * frames + first + t, 8, stride=PITCH), :] = total[
                        half * 8 : half * 8 + 8
                    ]

    def read_volts(first):
        def read(d, lane):
            start = pl.multiple_of((first + d) * FRAME, FRAME) + lane
            return volts[:, pl.ds(start, LANES)]

        return read

    def filter_blocks(low, high):
        @pl.loop(low, high)
        def _(b):
            first = pl.multiple_of(b * TAPS, TAPS)
            filter_frames(first, read_volts(first))

    halo_copy = pltpu.make_async_remote_copy(
        src_ref=v_hbm.at[:, pl.ds(frames * FRAME - HALO, HALO)],
        dst_ref=halo,
        send_sem=halo_send,
        recv_sem=halo_recv,
        device_id=(lax.axis_index("inputs"), lax.rem(block + 1, blocks)),
        device_id_type=MESH,
    )

    pl.semaphore_wait(barrier, len(x_peers + y_peers + z_peers))

    @pl.when(block < blocks - 1)
    def _():
        halo_copy.start()

    for peer in y_peers:
        pl.semaphore_signal(y_sem, inc=1, device_id=peer, device_id_type=MESH)
    per = chunk // TAPS
    load_taps.wait()
    load_volts[0].wait()
    filter_blocks(1, per)
    for c in range(1, CHUNKS):
        load_volts[c].wait()
        filter_blocks(c * per, (c + 1) * per)
    pl.semaphore_wait(y_sem, len(y_peers))
    for peer in x_peers:
        pl.semaphore_signal(x_sem, inc=1, device_id=peer, device_id_type=MESH)

    def round_frames(low, high):
        for pair in range(inp // 2):
            for half in range(2):
                to, src = (2 * pair + half) * frames, pair * PITCH + half * frames
                for part in range(FRAME // LANES):
                    filt[to + low : to + high, part * LANES : (part + 1) * LANES] = filt32[
                        part, src + low : src + high, :
                    ].astype(jnp.bfloat16)

    round_frames(2 * TAPS, frames)

    @pl.when(block > 0)
    def _():
        halo_copy.wait_recv()

    @pl.when(block == 0)
    def _():
        halo[...] = jnp.zeros_like(halo)

    def read_first(d, lane):
        if d < 0:
            return halo[:, (d + TAPS - 1) * FRAME + lane : (d + TAPS - 1) * FRAME + lane + LANES]
        return volts[:, d * FRAME + lane : d * FRAME + lane + LANES]

    filter_frames(0, read_first)
    round_frames(0, 2 * TAPS)
    load_table.wait()

    low = lax.broadcasted_iota(jnp.int32, (8, LANES), 1) < LANES // 2

    me = lax.axis_index("inputs")
    span = groups * inp
    slot = pl.multiple_of(me * inp, inp)

    def transform(j):
        owner = lax.rem(block + j, blocks)
        rows = table[pl.ds(pl.multiple_of(owner * 2 * groups, 2 * groups), 2 * groups), :]
        for q in range(4):
            quarter = slice(q * 256, (q + 1) * 256)
            spec = lax.dot_general(
                rows,
                filt[quarter, :],
                (((1,), (1,)), ((), ())),
                preferred_element_type=jnp.float32,
            )
            for u in range(2):
                pair = 2 * q + u
                for g in range(groups // 8):
                    re = spec[g * 8 : g * 8 + 8, u * LANES : (u + 1) * LANES]
                    im = spec[groups + g * 8 : groups + g * 8 + 8, u * LANES : (u + 1) * LANES]
                    first = jnp.where(low, re, pltpu.roll(im, LANES // 2, 1))
                    second = jnp.where(low, pltpu.roll(re, LANES // 2, 1), im)
                    base = g * 8 * inp + pair
                    stage[pl.ds(base, 8, stride=inp), :] = first
                    stage[pl.ds(base + 8, 8, stride=inp), :] = second
        send[j * span : (j + 1) * span, :] = stage[0:span, :].astype(jnp.bfloat16)

    def copy_to(j, device, row):
        return pltpu.make_async_remote_copy(
            src_ref=send.at[pl.ds(pl.multiple_of(j * span + row * inp, inp), inp)],
            dst_ref=early.at[pl.ds(j * span + slot, inp)]
            if j < EARLY
            else late.at[j - EARLY, pl.ds(slot, inp)],
            send_sem=send_sem,
            recv_sem=recv_sems.at[0 if j < EARLY else 1],
            device_id=device,
            device_id_type=MESH,
        )

    def send_range(j, low_step, high_step, turn):
        @pl.loop(low_step, high_step)
        def _(s):
            tx = lax.rem(x_hi + s // 32 + turn * (s // 4), 2)
            ty = lax.rem(y + s // 8 + s, 4)
            tz = lax.rem(z + s, 8)
            row = tx * 32 + ty * 8 + tz
            copy_to(j, (row, lax.rem(block + j, blocks)), row).start()

    for j in range(blocks):
        transform(j)
        if j == 0:
            send_range(j, 1, groups // 2, 0)
            early[pl.ds(slot, inp), :] = send[pl.ds(slot, inp), :]
        else:
            if j == 1:
                pl.semaphore_wait(x_sem, len(x_peers))
                send_range(0, groups // 2, groups, 0)
            send_range(j, 0, groups, 1)

    @pl.when(block < blocks - 1)
    def _():
        halo_copy.wait_send()

    def arrivals(ref, sem):
        return pltpu.make_async_remote_copy(
            src_ref=ref,
            dst_ref=ref,
            send_sem=send_sem,
            recv_sem=recv_sems.at[sem],
            device_id=(me, lax.rem(block + 1, blocks)),
            device_id_type=MESH,
        )

    arrivals(early.at[0 : EARLY * span - inp], 0).wait_recv()

    def keep(place, c, prod):
        sums[place // (36 // PARTS)][place % (36 // PARTS), c] = prod

    tile_products(
        [early.at[j * span : (j + 1) * span] for j in range(EARLY)], keep, lambda *_: None
    )

    arrivals(send.at[0 : blocks * span - inp], 1).wait_send()
    arrivals(late, 1).wait_recv()


def tile_products(specs, keep, done):
    count_in, lanes = specs[0].shape
    nt = count_in // TILE
    left = jnp.concatenate([spec[...] for spec in specs], axis=-1)
    sign = jnp.where(lax.broadcasted_iota(jnp.int32, (1, lanes), 1) < lanes // 2, 1.0, -1.0)
    side = 2 * TILE
    for big in range(nt // 2):
        rows = slice(big * side, (big + 1) * side)
        twisted = jnp.concatenate(
            [
                (pltpu.roll(spec[rows, :].astype(jnp.float32), lanes // 2, 1) * sign).astype(
                    jnp.bfloat16
                )
                for spec in specs
            ],
            axis=-1,
        )
        both = jnp.concatenate([left[rows], twisted], axis=0)
        for cb in range(big, nt // 2):
            prod = lax.dot_general(
                both,
                left[cb * side : (cb + 1) * side],
                (((1,), (1,)), ((), ())),
                preferred_element_type=jnp.float32,
            )
            for a in range(2):
                row = 2 * big + a
                first = max(row, 2 * cb)
                place = row * nt - row * (row - 1) // 2 + first - row
                for col in range(first, 2 * cb + 2):
                    b = col - 2 * cb
                    for c in range(2):
                        lo = c * side + a * TILE
                        keep(
                            place + col - first,
                            c,
                            prod[lo : lo + TILE, b * TILE : (b + 1) * TILE],
                        )
                done(place, place + 2 * cb + 2 - first)


def channelize(voltages, pfb_taps, table):
    inp, samples = voltages.shape
    frames = samples // FRAME
    rows = inp * frames
    return pl.pallas_call(
        functools.partial(channel_kernel, frames),
        out_shape=[jax.ShapeDtypeStruct((4 - EARLY, 64 * inp, LANES), jnp.bfloat16)]
        + [jax.ShapeDtypeStruct((36 // PARTS, 2, TILE, TILE), jnp.float32)] * PARTS,
        in_specs=[
            pl.BlockSpec(memory_space=pltpu.HBM),
            pl.BlockSpec(memory_space=pltpu.HBM),
            pl.BlockSpec(memory_space=pltpu.HBM),
        ],
        out_specs=[pl.BlockSpec(memory_space=pltpu.VMEM)] * (1 + PARTS),
        scratch_shapes=[
            pltpu.VMEM((inp, samples), jnp.bfloat16),
            pltpu.VMEM((TAPS, FRAME), jnp.float32),
            pltpu.VMEM((2 * F, FRAME), jnp.bfloat16),
            pltpu.VMEM((inp, HALO), jnp.bfloat16),
            pltpu.VMEM((FRAME // LANES, 8 * PITCH + 2 * frames, LANES), jnp.float32),
            pltpu.VMEM((rows, FRAME), jnp.bfloat16),
            pltpu.VMEM((64 * inp + inp, LANES), jnp.float32),
            pltpu.VMEM((4 * 64 * inp, LANES), jnp.bfloat16),
            pltpu.VMEM((EARLY * 64 * inp, LANES), jnp.bfloat16),
            pltpu.SemaphoreType.DMA((CHUNKS + 2,)),
            pltpu.SemaphoreType.DMA,
            pltpu.SemaphoreType.DMA,
            pltpu.SemaphoreType.DMA,
            pltpu.SemaphoreType.DMA((2,)),
            pltpu.SemaphoreType.REGULAR,
            pltpu.SemaphoreType.REGULAR,
        ],
        compiler_params=pltpu.CompilerParams(
            collective_id=0, has_side_effects=True, vmem_limit_bytes=VMEM_BYTES
        ),
    )(voltages, pfb_taps, table)


def tile_kernel(scale, late, *refs):
    sums = refs[:PARTS]
    out_hbm, tiles, sem = refs[PARTS:]
    copies = []

    def keep(place, c, prod):
        earlier = sums[place // (36 // PARTS)][place % (36 // PARTS), c]
        tiles[place, c] = (earlier + prod) * scale

    def done(low, high):
        copy = pltpu.make_async_copy(
            tiles.at[low:high], out_hbm.at[0, low:high], sem.at[len(copies)]
        )
        copy.start()
        copies.append(copy)

    tile_products([late.at[j] for j in range(late.shape[0])], keep, done)
    for copy in copies:
        copy.wait()


def tile_sums(late, sums, scale):
    nt = late.shape[1] // TILE
    pairs = nt * (nt + 1) // 2
    return pl.pallas_call(
        functools.partial(tile_kernel, scale),
        out_shape=jax.ShapeDtypeStruct((1, pairs, 2, TILE, TILE), jnp.float32),
        in_specs=[pl.BlockSpec(memory_space=pltpu.VMEM)] * (1 + PARTS),
        out_specs=pl.BlockSpec(memory_space=pl.ANY),
        scratch_shapes=[
            pltpu.VMEM((pairs, 2, TILE, TILE), jnp.float32),
            pltpu.SemaphoreType.DMA((nt // 2 * (nt // 2 + 1),)),
        ],
        compiler_params=pltpu.CompilerParams(vmem_limit_bytes=32 << 20),
    )(late, *sums)


def on_device(voltages, pfb_taps):
    table = jnp.asarray(dft_table(F, FRAME, lax.axis_size("tm")))
    frames = voltages.shape[1] // FRAME
    args = [pltpu.with_memory_space_constraint(a, pltpu.HBM) for a in (voltages, pfb_taps, table)]
    late, *sums = channelize(*args)
    return tile_sums(late, sums, 1.0 / (frames * lax.axis_size("tm")))


def solution(mesh):
    in_specs = (P("inputs", "tm"), P())
    out_specs = P(("inputs", "tm"), None, None, None, None)
    return jax.shard_map(
        on_device, mesh=mesh, in_specs=in_specs, out_specs=out_specs, check_vma=False
    )
```
